32 devices in a mesh: grp: 4 (over x, core), tile: 8 (over z, y).
Axes of the slice: x: 2, y: 2, z: 4, core: 2. Of those that a mesh axis runs over, the one named last changes fastest.
Arguments:
- tx_fields: bfloat16 [64, 8192], P(None, 'tile'), may hold values from -6 to 6
- rx_fields: bfloat16 [128, 8192], P(None, 'tile'), may hold values from -6 to 6
- layer_of_cell: int32 [8192], P('tile'), may hold values from 0 to 31
- layer_cond: float32 [32], replicated, may hold values from 0.05 to 5
- tx_of_row: int32 [1408], replicated, may hold values from 0 to 63
- rx_of_row: int32 [1408], replicated, may hold values from 0 to 127
- damping: float32 [1408], replicated, may hold values from 0.5 to 5
- panel_order: int32 [1408], replicated, may hold values from 0 to 1407, each once
Outputs:
- trailing: float32 [1408, 1408], P('grp', 'tile')
- factor: float32 [1408, 1024], P('grp')
The draws below stay inside these ranges and needn't reach their ends.
Inputs may be any that keep to these rules, and one draw needn't show every extreme that they name: `panel_order`: each data row appears exactly once; panel k is entries k * 512 to (k + 1) * 512 - 1.
All inputs are finite; a program needn't handle non-finite values.
Results may differ from the reference program's by a relative error of at most 0.0014.
Values may be sent and summed in bfloat16 or wider, within the bound.
No kernel may reach another device: no remote copies, remote signals or barrier semaphores. Data moves between devices by JAX's collectives and lax.ppermute only.
A program may use at most 64 MiB of HBM per device.

```python
import math
import jax
import jax.numpy as jnp
from jax import lax

NC = 1024
PANEL = 512
NPAN = 2
NTX = 64
NRX = 128
NLAYER = 32
M = 1408
NCELLS = 8192


def touch_ends(drawn, stream_key, least, top_value):
    spot = [jax.random.randint(jax.random.fold_in(stream_key, axis), (), 0, length) for axis, length in enumerate(drawn.shape)]
    longest = drawn.shape.index(max(drawn.shape))
    neighbour = spot[:longest] + [(spot[longest] + 1) % drawn.shape[longest]] + spot[longest + 1:]
    return drawn.at[tuple(spot)].set(least).at[tuple(neighbour)].set(top_value)


def steps_of(rng, dims, cuts, smallest, largest):
    def one(axis_at, shards_of):
        steps = jax.random.uniform(jax.random.fold_in(jax.random.fold_in(rng, 6), axis_at), (shards_of,), jnp.float32, smallest / len(cuts), largest / len(cuts))
        return jnp.repeat(jnp.exp(steps), dims[axis_at] // shards_of).reshape((-1,) + (1,) * (len(dims) - axis_at - 1))

    gain = one(*cuts[0])
    for cut in cuts[1:]:
        gain = gain * one(*cut)
    return gain


def gaussian(rng, shape, width, bound, shards=(), dtype=jnp.bfloat16):
    entries = jax.random.normal(rng, shape, jnp.float32) * width
    if len(shards) > 0:
        entries = steps_of(rng, shape, shards, -0.22, 0.18) * entries
    return jnp.clip(entries, min=-bound, max=bound).astype(dtype)


def setup_inputs(seed: int = 0) -> dict:
    seeds = jax.random.split(jax.random.key(seed), 9)
    tx_fields = gaussian(seeds[0], (NTX, NCELLS), 1.0, 6.0, ((1, 8),))
    rx_fields = gaussian(seeds[1], (NRX, NCELLS), 1.0, 6.0, ((1, 8),))
    layer_of_cell = touch_ends(jax.random.randint(seeds[2], (NCELLS,), 0, NLAYER), jax.random.fold_in(seeds[2], 1), 0, NLAYER - 1).astype(jnp.int32)
    layer_cond = jnp.clip(jnp.exp(jax.random.uniform(seeds[3], (NLAYER,), jnp.float32, math.log(0.05), math.log(5.0))), 0.05, 5.0)
    tx_of_row = touch_ends(jax.random.randint(seeds[4], (M,), 0, NTX), jax.random.fold_in(seeds[4], 1), 0, NTX - 1).astype(jnp.int32)
    rx_of_row = touch_ends(jax.random.randint(seeds[5], (M,), 0, NRX), jax.random.fold_in(seeds[5], 1), 0, NRX - 1).astype(jnp.int32)
    damping = jnp.clip(jnp.exp(jax.random.uniform(seeds[6], (M,), jnp.float32, math.log(0.5), math.log(5.0))), 0.5, 5.0)
    panel_order = jax.random.permutation(seeds[7], M).astype(jnp.int32)
    return {"tx_fields": tx_fields, "rx_fields": rx_fields, "layer_of_cell": layer_of_cell, "layer_cond": layer_cond, "tx_of_row": tx_of_row, "rx_of_row": rx_of_row, "damping": damping, "panel_order": panel_order}


highest = lax.Precision.HIGHEST

def reference(tx_fields, rx_fields, layer_of_cell, layer_cond, tx_of_row, rx_of_row, damping, panel_order):
    cell_cond = jnp.take(layer_cond, layer_of_cell, axis=0)
    block_count = NCELLS // NC
    tx_blocks = tx_fields.reshape(NTX, block_count, NC).transpose(1, 0, 2)
    rx_blocks = rx_fields.reshape(NRX, block_count, NC).transpose(1, 0, 2)
    cond_blocks = cell_cond.reshape(block_count, NC)

    def add_block(gram, block_inputs):
        tx_block, rx_block, cond_block = block_inputs
        sens = jnp.take(tx_block, tx_of_row, axis=0).astype(jnp.float32) * jnp.take(rx_block, rx_of_row, axis=0).astype(jnp.float32) * cond_block[None, :]
        sens = sens.astype(jnp.bfloat16)
        return (gram + jnp.dot(sens.astype(jnp.float32), sens.T.astype(jnp.float32), preferred_element_type=jnp.float32), None)
    gram = jnp.zeros((M, M), jnp.float32)
    gram, unused = lax.scan(add_block, gram, (tx_blocks, rx_blocks, cond_blocks))
    gram = gram / NCELLS + jnp.diag(damping)
    factor_parts = []
    for turn_index in range(NPAN):
        chosen = panel_order[turn_index * PANEL:(turn_index + 1) * PANEL]
        panel_columns = jnp.take(gram, chosen, axis=1)
        diag_block = jnp.take(panel_columns, chosen, axis=0)
        block_factor = jnp.linalg.cholesky(diag_block)
        panel_factor = lax.linalg.triangular_solve(block_factor, panel_columns, left_side=False, lower=True, transpose_a=True)
        gram = gram - jnp.dot(panel_factor, panel_factor.T, precision=highest)
        factor_parts.append(panel_factor)
    return (gram, jnp.concatenate(factor_parts, axis=1))
```

```python
import functools

import jax
import jax.numpy as jnp
from jax import lax
from jax.experimental import pallas as pl
from jax.experimental.pallas import tpu as pltpu
from jax.sharding import PartitionSpec as P

PANEL = 512
NPAN = 2
BLOCK = 128
STEP = 16
CHUNK = 512
PAD = 16


def halves(value):
    high = value.astype(jnp.bfloat16)
    low = (value - high.astype(jnp.float32)).astype(jnp.bfloat16)
    return high, low


def product(left, right, dims):
    def dot(a, b):
        return lax.dot_general(a, b, (dims, ((), ())), preferred_element_type=jnp.float32)

    return dot(left[0], right[0]) + (dot(left[0], right[1]) + dot(left[1], right[0]))


ROWS_ROWS = ((1,), (1,))
PLAIN = ((1,), (0,))


def factor_block(block, work, upper):
    size = block.shape[0]
    row = lax.broadcasted_iota(jnp.int32, (size, size), 0)
    col = lax.broadcasted_iota(jnp.int32, (size, size), 1)
    eye = (row == col).astype(jnp.float32)
    work[:, :size] = block
    work[:, size:] = eye
    sub = lax.broadcasted_iota(jnp.int32, (STEP, size), 0)
    wide = (STEP, size)
    rows0, rows1 = block[:STEP, :], eye[:STEP, :]
    for at in range(0, size, STEP):
        cols = [jnp.broadcast_to(rows0[:, at + k : at + k + 1], wide) for k in range(STEP)]
        more = at + STEP < size
        if more:
            after = work[at + STEP : at + 2 * STEP, :]
            after_cols = [jnp.broadcast_to(after[:, at + k : at + k + 1], wide) for k in range(STEP)]
        done0 = done1 = jnp.zeros(wide, jnp.float32)
        for j in range(STEP):
            pivot = jnp.broadcast_to(cols[j][j : j + 1, :], wide)
            ratio = (cols[j] - jnp.where(sub == j, 1.0, 0.0)) * (1.0 / pivot)
            root = lax.rsqrt(pivot)
            row0 = jnp.broadcast_to(rows0[j : j + 1, :], wide)
            row1 = jnp.broadcast_to(rows1[j : j + 1, :], wide)
            done0 = jnp.where(sub == j, row0 * root, done0)
            done1 = jnp.where(sub == j, row1 * root, done1)
            rows0 = rows0 - ratio * row0
            rows1 = rows1 - ratio * row1
            for k in range(j + 1, STEP):
                cols[k] = cols[k] - ratio * jnp.broadcast_to(cols[k][j : j + 1, :], wide)
        upper[at : at + STEP, :size] = done0
        upper[at : at + STEP, size:] = done1
        if not more:
            break
        terms0 = [after_cols[k] * jnp.broadcast_to(rows0[k : k + 1, :], wide) for k in range(STEP)]
        terms1 = [after_cols[k] * jnp.broadcast_to(rows1[k : k + 1, :], wide) for k in range(STEP)]
        while len(terms0) > 1:
            terms0 = [a + b for a, b in zip(terms0[::2], terms0[1::2])]
            terms1 = [a + b for a, b in zip(terms1[::2], terms1[1::2])]
        if at + 2 * STEP < size:
            solved = jnp.concatenate([rows0, rows1], axis=1)
            parts = [solved, jnp.zeros((size - at - STEP, 2 * size), jnp.float32)]
            if at > 0:
                parts.insert(0, jnp.zeros((at, 2 * size), jnp.float32))
            rest = work[at + 2 * STEP :, :]
            work[at + 2 * STEP :, :] = rest - product(
                halves(rest[:, :size]), halves(jnp.concatenate(parts, axis=0)), PLAIN
            )
        rows0 = after[:, :size] - terms0[0]
        rows1 = after[:, size:] - terms1[0]


def body(
    chosen_cols,
    cell_total,
    place,
    cells,
    hot,
    layer_cond,
    damping,
    order,
    trailing,
    factor,
    gram,
    sens,
    high,
    low,
    column,
    work,
    upper,
):
    rows = gram.shape[0]
    chunk = pl.program_id(0)
    ntx, nrx = hot.shape[1] - layer_cond.shape[1], layer_cond.shape[1]
    strips = [(a, min(a + 2 * BLOCK, rows)) for a in range(0, rows, 2 * BLOCK)]

    @pl.when(chunk == 0)
    def _():
        gram[...] = jnp.zeros_like(gram)

    nlayer = layer_cond.shape[0]
    layer = cells[0, ntx + nrx : ntx + nrx + 1, :].astype(jnp.float32)
    level = lax.broadcasted_iota(jnp.int32, (nlayer, layer.shape[1]), 0).astype(jnp.float32)
    cond = jnp.sum(jnp.where(level == layer, layer_cond[:, :1], 0.0), axis=0, keepdims=True)
    for a, b in strips:
        tx = jnp.dot(hot[a:b, :ntx], cells[0, :ntx, :], preferred_element_type=jnp.float32)
        rx = jnp.dot(hot[a:b, ntx:], cells[0, ntx : ntx + nrx, :], preferred_element_type=jnp.float32)
        sens[a:b, :] = (tx * rx * cond).astype(jnp.bfloat16)
        gram[a:b, :b] += lax.dot_general(
            sens[a:b, :], sens[:b, :], (ROWS_ROWS, ((), ())), preferred_element_type=jnp.float32
        )

    @pl.when(chunk == pl.num_programs(0) - 1)
    def _():
        finish(
            chosen_cols, cell_total, place, damping, order, trailing, factor,
            gram, high, low, column, work, upper,
        )


def finish(
    chosen_cols, cell_total, place, damping, order, trailing, factor, gram, high, low, column, work, upper
):
    rows = gram.shape[0]
    scale = 1.0 / cell_total
    row = lax.broadcasted_iota(jnp.int32, (BLOCK, BLOCK), 0)
    col = lax.broadcasted_iota(jnp.int32, (BLOCK, BLOCK), 1)
    for at in range(0, chosen_cols, BLOCK):
        end = at + BLOCK
        column[at:, :] = gram[at:, at:end] * scale
        column[at:end, :] += jnp.where(row == col, damping[:, at:end], 0.0)
        if at > 0:
            column[at:, :] -= product(
                (high[at:, :at], low[at:, :at]), (high[at:end, :at], low[at:end, :at]), ROWS_ROWS
            )
            high[:at, at:end] = jnp.zeros((at, BLOCK), jnp.bfloat16)
            low[:at, at:end] = jnp.zeros((at, BLOCK), jnp.bfloat16)
        factor_block(column[at:end, :], work, upper)
        h, l = halves(jnp.where(row >= col, upper[:, :BLOCK].T, 0.0))
        high[at:end, at:end] = h
        low[at:end, at:end] = l
        inverse = halves(upper[:, BLOCK:])
        h, l = halves(product(halves(column[end:, :]), inverse, ROWS_ROWS))
        high[end:, at:end] = h
        low[end:, at:end] = l

    group_rows, tile_cols = trailing.shape
    row_hot = (
        place[0] + lax.broadcasted_iota(jnp.int32, (group_rows, rows), 0) == order[...]
    ).astype(jnp.bfloat16)
    factor[...] = jnp.dot(row_hot, high[...], preferred_element_type=jnp.float32) + jnp.dot(
        row_hot, low[...], preferred_element_type=jnp.float32
    )
    left = rows - chosen_cols
    col_hot = (
        place[1] + lax.broadcasted_iota(jnp.int32, (tile_cols, left), 0) == order[:, chosen_cols:]
    ).astype(jnp.bfloat16)
    row_hot = row_hot[:, chosen_cols:]
    damp_left = damping[:, chosen_cols:]
    picked = []
    for a in range(0, left, BLOCK):
        b = min(a + BLOCK, left)
        at, end = chosen_cols + a, chosen_cols + b
        ids = lax.broadcasted_iota(jnp.int32, (left, b - a), 0)
        across = a + lax.broadcasted_iota(jnp.int32, (left, b - a), 1)
        lower = gram[chosen_cols:, at:end]
        strip = lower
        if a > 0:
            strip = jnp.concatenate([gram[at:end, chosen_cols:at].T, lower[a:]], axis=0)
        strip = strip * scale + jnp.where(ids == across, damp_left[:, a:b], 0.0)
        strip = strip - product(
            (high[chosen_cols:, :], low[chosen_cols:, :]), (high[at:end, :], low[at:end, :]), ROWS_ROWS
        )
        h, l = halves(strip)
        picked.append(
            jnp.dot(row_hot, h, preferred_element_type=jnp.float32)
            + jnp.dot(row_hot, l, preferred_element_type=jnp.float32)
        )
    h, l = halves(jnp.concatenate(picked, axis=1))
    trailing[...] = lax.dot_general(
        h, col_hot, (ROWS_ROWS, ((), ())), preferred_element_type=jnp.float32
    ) + lax.dot_general(l, col_hot, (ROWS_ROWS, ((), ())), preferred_element_type=jnp.float32)


def shards(
    tx_fields, rx_fields, layer_of_cell, layer_cond, tx_of_row, rx_of_row, damping, panel_order
):
    grp_count = lax.axis_size("grp")
    tile_count = lax.axis_size("tile")
    tile_cells = tx_fields.shape[1]
    ntx, nrx = tx_fields.shape[0], rx_fields.shape[0]
    rows = tx_of_row.shape[0]
    group_rows = rows // grp_count
    tile_cols = rows // tile_count
    grp, tile = lax.axis_index("grp"), lax.axis_index("tile")

    layers = jnp.broadcast_to(layer_of_cell.astype(jnp.bfloat16)[None, :], (PAD, tile_cells))
    own = jnp.concatenate([tx_fields, rx_fields, layers], axis=0)
    half = tile_cells // 2
    mine = lax.dynamic_slice_in_dim(own, (grp % 2) * half, half, axis=1)
    got = [
        lax.ppermute(mine, "tile", [(i, (i + k) % tile_count) for i in range(tile_count)])
        for k in range(1, tile_count)
    ]
    got = jnp.stack(got)
    other = lax.ppermute(got, "grp", [(i, i ^ 1) for i in range(grp_count)])
    cells = jnp.concatenate([jnp.stack([own[:, :half], own[:, half:]]), got, other], axis=0)

    tx_ids = jnp.take(tx_of_row, panel_order)
    rx_ids = jnp.take(rx_of_row, panel_order)
    damp = jnp.take(damping, panel_order)
    hot = jnp.concatenate(
        [
            tx_ids[:, None] == jnp.arange(ntx, dtype=jnp.int32)[None, :],
            rx_ids[:, None] == jnp.arange(nrx, dtype=jnp.int32)[None, :],
        ],
        axis=1,
    ).astype(jnp.bfloat16)
    place = jnp.stack([grp * group_rows, tile * tile_cols]).astype(jnp.int32)
    chosen_cols = PANEL * NPAN
    vmem = pl.BlockSpec(memory_space=pltpu.VMEM)
    call = pl.pallas_call(
        functools.partial(body, chosen_cols, tile_cells * tile_count),
        grid=(cells.shape[0],),
        in_specs=[
            pl.BlockSpec(memory_space=pltpu.SMEM),
            pl.BlockSpec((1,) + cells.shape[1:], lambda i: (i, 0, 0)),
            vmem, vmem, vmem, vmem,
        ],
        out_specs=[vmem, vmem],
        out_shape=[
            jax.ShapeDtypeStruct((group_rows, tile_cols), jnp.float32),
            jax.ShapeDtypeStruct((group_rows, chosen_cols), jnp.float32),
        ],
        scratch_shapes=[
            pltpu.VMEM((rows, rows), jnp.float32),
            pltpu.VMEM((rows, half), jnp.bfloat16),
            pltpu.VMEM((rows, chosen_cols), jnp.bfloat16),
            pltpu.VMEM((rows, chosen_cols), jnp.bfloat16),
            pltpu.VMEM((rows, BLOCK), jnp.float32),
            pltpu.VMEM((BLOCK, 2 * BLOCK), jnp.float32),
            pltpu.VMEM((BLOCK, 2 * BLOCK), jnp.float32),
        ],
        compiler_params=pltpu.CompilerParams(vmem_limit_bytes=60 * 2**20),
    )
    return tuple(
        call(
            place,
            cells,
            hot,
            jnp.broadcast_to(layer_cond[:, None], (layer_cond.shape[0], nrx)),
            damp[None, :],
            panel_order[None, :],
        )
    )


def solution(mesh):
    placed = (P(None, "tile"), P(None, "tile"), P("tile"), P(), P(), P(), P(), P())
    return jax.shard_map(
        shards,
        mesh=mesh,
        in_specs=placed,
        out_specs=(P("grp", "tile"), P("grp", None)),
        check_vma=False,
    )
```

```python
import functools

import jax
import jax.numpy as jnp
from jax import lax
from jax.experimental import pallas as pl
from jax.experimental.pallas import tpu as pltpu
from jax.sharding import PartitionSpec as P

PANEL = 512
NPAN = 2
BLOCK = 128
STEP = 16
STRIP = 256
GROUP = 3
PAD = 16
VMEM = pl.BlockSpec(memory_space=pltpu.VMEM)
SMEM = pl.BlockSpec(memory_space=pltpu.SMEM)
ROWS_ROWS = ((1,), (1,))
PLAIN = ((1,), (0,))


def grant(*shapes):
    total = 0
    for shape, width in shapes:
        size = width
        for axis in shape:
            size *= axis
        total += size
    return min(60 * 2**20, total + total // 8 + 6 * 2**20)


def halves(value):
    high = value.astype(jnp.bfloat16)
    low = (value - high.astype(jnp.float32)).astype(jnp.bfloat16)
    return high, low


def dot(a, b, dims):
    return lax.dot_general(a, b, (dims, ((), ())), preferred_element_type=jnp.float32)


def product(left, right, dims):
    return dot(left[0], right[0], dims) + (dot(left[0], right[1], dims) + dot(left[1], right[0], dims))


def factor_block(block, work, upper):
    size = block.shape[0]
    row = lax.broadcasted_iota(jnp.int32, (size, size), 0)
    col = lax.broadcasted_iota(jnp.int32, (size, size), 1)
    eye = (row == col).astype(jnp.float32)
    work[:, :size] = block
    work[:, size:] = eye
    sub = lax.broadcasted_iota(jnp.int32, (STEP, size), 0)
    wide = (STEP, size)
    rows0, rows1 = block[:STEP, :], eye[:STEP, :]
    for at in range(0, size, STEP):
        cols = [jnp.broadcast_to(rows0[:, at + k : at + k + 1], wide) for k in range(STEP)]
        more = at + STEP < size
        if more:
            after = work[at + STEP : at + 2 * STEP, :]
            after_cols = [jnp.broadcast_to(after[:, at + k : at + k + 1], wide) for k in range(STEP)]
        done0 = done1 = jnp.zeros(wide, jnp.float32)
        for j in range(STEP):
            pivot = jnp.broadcast_to(cols[j][j : j + 1, :], wide)
            ratio = (cols[j] - jnp.where(sub == j, 1.0, 0.0)) * (1.0 / pivot)
            root = lax.rsqrt(pivot)
            row0 = jnp.broadcast_to(rows0[j : j + 1, :], wide)
            row1 = jnp.broadcast_to(rows1[j : j + 1, :], wide)
            done0 = jnp.where(sub == j, row0 * root, done0)
            done1 = jnp.where(sub == j, row1 * root, done1)
            rows0 = rows0 - ratio * row0
            rows1 = rows1 - ratio * row1
            for k in range(j + 1, STEP):
                cols[k] = cols[k] - ratio * jnp.broadcast_to(cols[k][j : j + 1, :], wide)
        upper[at : at + STEP, :size] = done0
        upper[at : at + STEP, size:] = done1
        if not more:
            break
        terms0 = [after_cols[k] * jnp.broadcast_to(rows0[k : k + 1, :], wide) for k in range(STEP)]
        terms1 = [after_cols[k] * jnp.broadcast_to(rows1[k : k + 1, :], wide) for k in range(STEP)]
        while len(terms0) > 1:
            terms0 = [a + b for a, b in zip(terms0[::2], terms0[1::2])]
            terms1 = [a + b for a, b in zip(terms1[::2], terms1[1::2])]
        if at + 2 * STEP < size:
            solved = jnp.concatenate([rows0, rows1], axis=1)
            parts = [solved, jnp.zeros((size - at - STEP, 2 * size), jnp.float32)]
            if at > 0:
                parts.insert(0, jnp.zeros((at, 2 * size), jnp.float32))
            rest = work[at + 2 * STEP :, :]
            work[at + 2 * STEP :, :] = rest - product(
                halves(rest[:, :size]), halves(jnp.concatenate(parts, axis=0)), PLAIN
            )
        rows0 = after[:, :size] - terms0[0]
        rows1 = after[:, size:] - terms1[0]


def strips_of(rows):
    return [(a, min(a + STRIP, rows)) for a in range(0, rows, STRIP)]


def select_body(ntx, nrx, order, tx_of_row, rx_of_row, damping, hot, damp, table):
    rows = order.shape[1]
    table[:ntx, :] = (
        lax.broadcasted_iota(jnp.int32, (ntx, rows), 0) == tx_of_row[...]
    ).astype(jnp.bfloat16)
    table[ntx : ntx + nrx, :] = (
        lax.broadcasted_iota(jnp.int32, (nrx, rows), 0) == rx_of_row[...]
    ).astype(jnp.bfloat16)
    spare = table.shape[0] - ntx - nrx
    high = damping[...].astype(jnp.bfloat16).astype(jnp.float32)
    middle, low = halves(damping[...] - high)
    which = lax.broadcasted_iota(jnp.int32, (spare, rows), 0)
    table[ntx + nrx :, :] = (
        jnp.where(which == 0, high, 0.0)
        + jnp.where(which == 1, middle.astype(jnp.float32), 0.0)
        + jnp.where(which == 2, low.astype(jnp.float32), 0.0)
    ).astype(jnp.bfloat16)
    for a, b in strips_of(rows):
        pick = (
            lax.broadcasted_iota(jnp.int32, (rows, b - a), 0) == order[:, a:b]
        ).astype(jnp.bfloat16)
        found = dot(table[...], pick, PLAIN)
        hot[a:b, :] = found.T.astype(jnp.bfloat16)
        damp[:, a:b] = jnp.sum(found[ntx + nrx :, :], axis=0, keepdims=True)


def gram_body(ntx, nrx, count, stacked, first, hot, layer_cond, *refs):
    held = 1 if stacked else count
    blocks, refs = refs[:held], refs[held:]
    rows = hot.shape[0]
    strips = strips_of(rows)
    before = () if first else refs[: len(strips)]
    after = refs[len(before) : len(before) + len(strips)]
    sens = refs[-1]
    nlayer = layer_cond.shape[0]
    size = blocks[0].shape[-1]

    def sensitivities(cells, at):
        layer = cells[ntx + nrx : ntx + nrx + 1, :].astype(jnp.float32)
        level = lax.broadcasted_iota(jnp.int32, (nlayer, size), 0).astype(jnp.float32)
        cond = jnp.sum(jnp.where(level == layer, layer_cond[:, :1], 0.0), axis=0, keepdims=True)
        for a, b in strips:
            tx = dot(hot[a:b, :ntx], cells[:ntx, :], PLAIN)
            rx = dot(hot[a:b, ntx : ntx + nrx], cells[ntx : ntx + nrx, :], PLAIN)
            sens[a:b, at : at + size] = (tx * rx * cond).astype(jnp.bfloat16)

    def add(source, depth):
        for s, (a, b) in enumerate(strips):
            part = dot(sens[a:, :depth], sens[a:b, :depth], ROWS_ROWS)
            after[s][...] = part if source is None else source[s][...] + part

    if stacked:
        for s in range(len(strips)):
            after[s][...] = jnp.zeros_like(after[s]) if first else before[s][...]

        def one(i, carry):
            sensitivities(blocks[0].at[i], 0)
            add(after, size)
            return carry

        lax.fori_loop(0, count, one, 0)
        return
    source = None if first else before
    for start in range(0, count, GROUP):
        group = blocks[start : start + GROUP]
        for i, cells in enumerate(group):
            sensitivities(cells, i * size)
        add(source, len(group) * size)
        source = after


def finish_body(chosen_cols, cell_total, count, place, damping, order, *refs):
    mine, refs = refs[:count], refs[count:]
    theirs, refs = refs[:count], refs[count:]
    trailing, factor, high, low, column, work, upper = refs
    rows = high.shape[0]
    scale = 1.0 / cell_total
    row = lax.broadcasted_iota(jnp.int32, (BLOCK, BLOCK), 0)
    col = lax.broadcasted_iota(jnp.int32, (BLOCK, BLOCK), 1)

    def gram(a, at, end):
        s = at // STRIP
        base = s * STRIP
        part = (slice(a - base, None), slice(at - base, end - base))
        return (mine[s][part] + theirs[s][part]) * scale

    for at in range(0, chosen_cols, BLOCK):
        end = at + BLOCK
        column[at:, :] = gram(at, at, end)
        column[at:end, :] += jnp.where(row == col, damping[:, at:end], 0.0)
        if at > 0:
            column[at:, :] -= product(
                (high[at:, :at], low[at:, :at]), (high[at:end, :at], low[at:end, :at]), ROWS_ROWS
            )
        above = at - at % STRIP
        if above < at:
            high[above:at, at:end] = jnp.zeros((at - above, BLOCK), jnp.bfloat16)
            low[above:at, at:end] = jnp.zeros((at - above, BLOCK), jnp.bfloat16)
        factor_block(column[at:end, :], work, upper)
        h, l = halves(jnp.where(row >= col, upper[:, :BLOCK].T, 0.0))
        high[at:end, at:end] = h
        low[at:end, at:end] = l
        inverse = halves(upper[:, BLOCK:])
        h, l = halves(product(halves(column[end:, :]), inverse, ROWS_ROWS))
        high[end:, at:end] = h
        low[end:, at:end] = l

    group_rows, tile_cols = trailing.shape
    row_hot = (
        place[0] + lax.broadcasted_iota(jnp.int32, (group_rows, rows), 0) == order[...]
    ).astype(jnp.bfloat16)
    col_hot = (
        place[1]
        + lax.broadcasted_iota(jnp.int32, (tile_cols, rows - chosen_cols), 0)
        == order[:, chosen_cols:]
    ).astype(jnp.bfloat16)
    left_hot = row_hot[:, chosen_cols:]
    total = jnp.zeros((group_rows, tile_cols), jnp.float32)
    kept = jnp.sum(left_hot.astype(jnp.float32), axis=1, keepdims=True)
    for at in range(0, chosen_cols, STRIP):
        end = at + STRIP
        rows_high = dot(row_hot[:, at:], high[at:, at:end], PLAIN)
        rows_low = dot(row_hot[:, at:], low[at:, at:end], PLAIN)
        factor[:, at:end] = rows_high + rows_low
        cols_high = dot(col_hot, high[chosen_cols:, at:end], PLAIN)
        cols_low = dot(col_hot, low[chosen_cols:, at:end], PLAIN)
        total -= product(
            ((rows_high * kept).astype(jnp.bfloat16), (rows_low * kept).astype(jnp.bfloat16)),
            (cols_high.astype(jnp.bfloat16), cols_low.astype(jnp.bfloat16)),
            ROWS_ROWS,
        )
    for at in range(chosen_cols, rows, STRIP):
        end = min(at + STRIP, rows)
        ids = lax.broadcasted_iota(jnp.int32, (rows - at, end - at), 0)
        across = lax.broadcasted_iota(jnp.int32, (rows - at, end - at), 1)
        strip = gram(at, at, end) + jnp.where(ids == across, damping[:, at:end], 0.0)
        a, b = at - chosen_cols, end - chosen_cols
        for value in halves(strip):
            some = dot(left_hot[:, a:], value, PLAIN).astype(jnp.bfloat16)
            total += dot(some, col_hot[:, a:b], ROWS_ROWS)
            if end < rows:
                some = dot(left_hot[:, a:b], value[b - a :, :], ROWS_ROWS).astype(jnp.bfloat16)
                total += dot(some, col_hot[:, b:], ROWS_ROWS)
    trailing[...] = total


def shards(
    tx_fields, rx_fields, layer_of_cell, layer_cond, tx_of_row, rx_of_row, damping, panel_order
):
    grp_count = lax.axis_size("grp")
    tile_count = lax.axis_size("tile")
    tile_cells = tx_fields.shape[1]
    ntx, nrx = tx_fields.shape[0], rx_fields.shape[0]
    rows = tx_of_row.shape[0]
    group_rows = rows // grp_count
    tile_cols = rows // tile_count
    chosen_cols = PANEL * NPAN
    grp, tile = lax.axis_index("grp"), lax.axis_index("tile")

    half = tile_cells // 2
    start = (grp % 2) * half

    def piece(x):
        return lax.dynamic_slice_in_dim(x, start, half, axis=x.ndim - 1)

    own = jnp.concatenate(
        [
            piece(tx_fields),
            piece(rx_fields),
            jnp.broadcast_to(piece(layer_of_cell).astype(jnp.bfloat16)[None, :], (PAD, half)),
        ],
        axis=0,
    )

    inner = 1
    while inner * inner * 4 <= tile_count:
        inner *= 2
    outer = tile_count // inner

    def along(value, step):
        pairs = []
        for i in range(tile_count):
            o, n = divmod(i, inner)
            o = o ^ step[0] if outer & (outer - 1) == 0 else (o + step[0]) % outer
            n = n ^ step[1] if inner & (inner - 1) == 0 else (n + step[1]) % inner
            pairs.append((i, o * inner + n))
        return lax.ppermute(value, "tile", pairs)

    near = [along(own, (0, k)) for k in range(1, inner)]
    far = [along(own, (k, 0)) for k in range(1, outer)]
    relayed = [[along(value, (0, k)) for k in range(1, inner)] for value in far]
    groups = [
        [own] + near + far[:1],
        far[1:] + relayed[0],
        [value for values in relayed[1:] for value in values],
    ]

    line = lambda x: x[None, :]
    width = -(-(ntx + nrx + 3) // BLOCK) * BLOCK
    hot, damp = pl.pallas_call(
        functools.partial(select_body, ntx, nrx),
        in_specs=[VMEM] * 4,
        out_specs=[VMEM] * 2,
        out_shape=[
            jax.ShapeDtypeStruct((rows, width), jnp.bfloat16),
            jax.ShapeDtypeStruct((1, rows), jnp.float32),
        ],
        scratch_shapes=[pltpu.VMEM((width, rows), jnp.bfloat16)],
        compiler_params=pltpu.CompilerParams(
            vmem_limit_bytes=grant(((rows, width), 8), ((rows, STRIP), 8))
        ),
        cost_estimate=pl.CostEstimate(
            flops=2 * width * rows * rows, bytes_accessed=4 * rows * width, transcendentals=0
        ),
    )(line(panel_order), line(tx_of_row), line(rx_of_row), line(damping))

    strips = strips_of(rows)
    strip_shapes = [jax.ShapeDtypeStruct((rows - a, b - a), jnp.float32) for a, b in strips]
    lower = sum((rows - a) * (b - a) for a, b in strips)
    conds = jnp.broadcast_to(layer_cond[:, None], (layer_cond.shape[0], BLOCK))
    sums = []
    for blocks in groups:
        if not blocks:
            continue
        count = len(blocks)
        stacked = count > GROUP
        depth = half * (1 if stacked else min(count, GROUP))
        args = [jnp.stack(blocks)] if stacked else blocks
        sums = pl.pallas_call(
            functools.partial(gram_body, ntx, nrx, count, stacked, not sums),
            in_specs=[VMEM] * (2 + len(args) + len(sums)),
            out_specs=[VMEM] * len(strips),
            out_shape=strip_shapes,
            scratch_shapes=[pltpu.VMEM((rows, depth), jnp.bfloat16)],
            input_output_aliases={2 + len(args) + i: i for i in range(len(sums))},
            compiler_params=pltpu.CompilerParams(
                vmem_limit_bytes=grant(
                    ((lower,), 8), ((rows, depth), 2), ((rows, width), 2), ((count, own.size), 2)
                )
            ),
            cost_estimate=pl.CostEstimate(
                flops=2 * count * half * (lower + rows * STRIP * 2),
                bytes_accessed=8 * lower,
                transcendentals=0,
            ),
        )(hot, conds, *args, *sums)
    theirs = [lax.ppermute(s, "grp", [(i, i ^ 1) for i in range(grp_count)]) for s in sums]

    place = jnp.stack([grp * group_rows, tile * tile_cols]).astype(jnp.int32)
    return tuple(
        pl.pallas_call(
            functools.partial(finish_body, chosen_cols, tile_cells * tile_count, len(strips)),
            in_specs=[SMEM] + [VMEM] * (2 + 2 * len(strips)),
            out_specs=[VMEM, VMEM],
            out_shape=[
                jax.ShapeDtypeStruct((group_rows, tile_cols), jnp.float32),
                jax.ShapeDtypeStruct((group_rows, chosen_cols), jnp.float32),
            ],
            scratch_shapes=[
                pltpu.VMEM((rows, chosen_cols), jnp.bfloat16),
                pltpu.VMEM((rows, chosen_cols), jnp.bfloat16),
                pltpu.VMEM((rows, BLOCK), jnp.float32),
                pltpu.VMEM((BLOCK, 2 * BLOCK), jnp.float32),
                pltpu.VMEM((BLOCK, 2 * BLOCK), jnp.float32),
            ],
            compiler_params=pltpu.CompilerParams(
                vmem_limit_bytes=grant(
                    ((lower,), 8), ((rows, chosen_cols), 4), ((rows, BLOCK), 16),
                    ((group_rows, chosen_cols + STRIP), 4), ((group_rows, rows), 2),
                )
            ),
            cost_estimate=pl.CostEstimate(
                flops=6 * rows * rows * chosen_cols, bytes_accessed=8 * lower, transcendentals=0
            ),
        )(place, damp, line(panel_order), *sums, *theirs)
    )


def solution(mesh):
    placed = (P(None, "tile"), P(None, "tile"), P("tile"), P(), P(), P(), P(), P())
    return jax.shard_map(
        shards,
        mesh=mesh,
        in_specs=placed,
        out_specs=(P("grp", "tile"), P("grp", None)),
        check_vma=False,
    )
```

```python
import functools

import jax
import jax.numpy as jnp
from jax import lax
from jax.experimental import pallas as pl
from jax.experimental.pallas import tpu as pltpu
from jax.sharding import PartitionSpec as P

PANEL = 512
NPAN = 2
BLOCK = 128
STEP = 16
STRIP = 256
GROUP = 3
PAD = 16
VMEM = pl.BlockSpec(memory_space=pltpu.VMEM)
SMEM = pl.BlockSpec(memory_space=pltpu.SMEM)
ROWS_ROWS = ((1,), (1,))
PLAIN = ((1,), (0,))


def grant(*shapes):
    total = 0
    for shape, width in shapes:
        size = width
        for axis in shape:
            size *= axis
        total += size
    return min(60 * 2**20, total + total // 8 + 6 * 2**20)


def halves(value):
    high = value.astype(jnp.bfloat16)
    low = (value - high.astype(jnp.float32)).astype(jnp.bfloat16)
    return high, low


def dot(a, b, dims):
    return lax.dot_general(a, b, (dims, ((), ())), preferred_element_type=jnp.float32)


def product(left, right, dims):
    return dot(left[0], right[0], dims) + (dot(left[0], right[1], dims) + dot(left[1], right[0], dims))


def factor_block(block, work, upper, beside=()):
    size = block.shape[0]
    row = lax.broadcasted_iota(jnp.int32, (size, size), 0)
    col = lax.broadcasted_iota(jnp.int32, (size, size), 1)
    eye = (row == col).astype(jnp.float32)
    work[:, :size] = block
    work[:, size:] = eye
    sub = lax.broadcasted_iota(jnp.int32, (STEP, size), 0)
    wide = (STEP, size)
    rows0, rows1 = block[:STEP, :], eye[:STEP, :]
    for at in range(0, size, STEP):
        cols = [jnp.broadcast_to(rows0[:, at + k : at + k + 1], wide) for k in range(STEP)]
        for call in beside[at * len(beside) // size : (at + STEP) * len(beside) // size]:
            call()
        more = at + STEP < size
        if more:
            after = work[at + STEP : at + 2 * STEP, :]
            after_cols = [jnp.broadcast_to(after[:, at + k : at + k + 1], wide) for k in range(STEP)]
        done0 = done1 = jnp.zeros(wide, jnp.float32)
        for j in range(STEP):
            pivot = jnp.broadcast_to(cols[j][j : j + 1, :], wide)
            ratio = (cols[j] - jnp.where(sub == j, 1.0, 0.0)) * (1.0 / pivot)
            root = lax.rsqrt(pivot)
            row0 = jnp.broadcast_to(rows0[j : j + 1, :], wide)
            row1 = jnp.broadcast_to(rows1[j : j + 1, :], wide)
            done0 = jnp.where(sub == j, row0 * root, done0)
            done1 = jnp.where(sub == j, row1 * root, done1)
            rows0 = rows0 - ratio * row0
            rows1 = rows1 - ratio * row1
            for k in range(j + 1, STEP):
                cols[k] = cols[k] - ratio * jnp.broadcast_to(cols[k][j : j + 1, :], wide)
        upper[at : at + STEP, :size] = done0
        upper[at : at + STEP, size:] = done1
        if not more:
            break
        terms0 = [after_cols[k] * jnp.broadcast_to(rows0[k : k + 1, :], wide) for k in range(STEP)]
        terms1 = [after_cols[k] * jnp.broadcast_to(rows1[k : k + 1, :], wide) for k in range(STEP)]
        while len(terms0) > 1:
            terms0 = [a + b for a, b in zip(terms0[::2], terms0[1::2])]
            terms1 = [a + b for a, b in zip(terms1[::2], terms1[1::2])]
        if at + 2 * STEP < size:
            solved = jnp.concatenate([rows0, rows1], axis=1)
            parts = [solved, jnp.zeros((size - at - STEP, 2 * size), jnp.float32)]
            if at > 0:
                parts.insert(0, jnp.zeros((at, 2 * size), jnp.float32))
            rest = work[at + 2 * STEP :, :]
            work[at + 2 * STEP :, :] = rest - product(
                halves(rest[:, :size]), halves(jnp.concatenate(parts, axis=0)), PLAIN
            )
        rows0 = after[:, :size] - terms0[0]
        rows1 = after[:, size:] - terms1[0]


def strips_of(rows):
    return [(a, min(a + STRIP, rows)) for a in range(0, rows, STRIP)]


def select_body(ntx, nrx, order, tx_of_row, rx_of_row, damping, hot, damp, table):
    rows = order.shape[1]
    table[:ntx, :] = (
        lax.broadcasted_iota(jnp.int32, (ntx, rows), 0) == tx_of_row[...]
    ).astype(jnp.bfloat16)
    table[ntx : ntx + nrx, :] = (
        lax.broadcasted_iota(jnp.int32, (nrx, rows), 0) == rx_of_row[...]
    ).astype(jnp.bfloat16)
    spare = table.shape[0] - ntx - nrx
    high = damping[...].astype(jnp.bfloat16).astype(jnp.float32)
    middle, low = halves(damping[...] - high)
    which = lax.broadcasted_iota(jnp.int32, (spare, rows), 0)
    table[ntx + nrx :, :] = (
        jnp.where(which == 0, high, 0.0)
        + jnp.where(which == 1, middle.astype(jnp.float32), 0.0)
        + jnp.where(which == 2, low.astype(jnp.float32), 0.0)
    ).astype(jnp.bfloat16)
    for a, b in strips_of(rows):
        pick = (
            lax.broadcasted_iota(jnp.int32, (rows, b - a), 0) == order[:, a:b]
        ).astype(jnp.bfloat16)
        found = dot(table[...], pick, PLAIN)
        hot[a:b, :] = found.T.astype(jnp.bfloat16)
        damp[:, a:b] = jnp.sum(found[ntx + nrx :, :], axis=0, keepdims=True)


def rest_body(depth, strips, sens, *refs):
    for s, (a, b) in enumerate(strips):
        refs[len(strips) + s][...] = refs[s][...] + dot(sens[a:, :], sens[a:b, :], ROWS_ROWS)


def gram_body(ntx, nrx, count, stacked, first, some, hot, layer_cond, *refs):
    held = 1 if stacked else count
    blocks, refs = refs[:held], refs[held:]
    rows = hot.shape[0]
    bands = strips_of(rows)
    strips = bands[:some]
    before = () if first else refs[: len(strips)]
    after = refs[len(before) : len(before) + len(strips)]
    sens = refs[-1]
    nlayer = layer_cond.shape[0]
    size = blocks[0].shape[-1]

    def sensitivities(cells, at):
        layer = cells[ntx + nrx : ntx + nrx + 1, :].astype(jnp.float32)
        level = lax.broadcasted_iota(jnp.int32, (nlayer, size), 0).astype(jnp.float32)
        cond = jnp.sum(jnp.where(level == layer, layer_cond[:, :1], 0.0), axis=0, keepdims=True)
        for a, b in bands:
            tx = dot(hot[a:b, :ntx], cells[:ntx, :], PLAIN)
            rx = dot(hot[a:b, ntx : ntx + nrx], cells[ntx : ntx + nrx, :], PLAIN)
            sens[a:b, at : at + size] = (tx * rx * cond).astype(jnp.bfloat16)

    def add(source, depth):
        for s, (a, b) in enumerate(strips):
            part = dot(sens[a:, :depth], sens[a:b, :depth], ROWS_ROWS)
            after[s][...] = part if source is None else source[s][...] + part

    if stacked:
        for s in range(len(strips)):
            after[s][...] = jnp.zeros_like(after[s]) if first else before[s][...]

        def one(i, carry):
            sensitivities(blocks[0].at[i], 0)
            add(after, size)
            return carry

        lax.fori_loop(0, count, one, 0)
        return
    source = None if first else before
    for start in range(0, count, GROUP):
        group = blocks[start : start + GROUP]
        for i, cells in enumerate(group):
            sensitivities(cells, i * size)
        add(source, len(group) * size)
        source = after


class Panels:
    def __init__(self, pairs):
        self.pairs = pairs

    def of(self, k, a, b):
        s, c = divmod(k * BLOCK, STRIP)
        part = (slice(a - s * STRIP, b - s * STRIP), slice(c, c + BLOCK))
        return tuple(ref.at[part] for ref in self.pairs[s])

    def put(self, k, a, b, pair):
        for ref, value in zip(self.of(k, a, b), pair):
            ref[...] = value

    def sums(self, a, b, c, d, count):
        total = None
        for start in range(0, count * BLOCK, STRIP):
            s, width = start // STRIP, min(STRIP, count * BLOCK - start)
            high, low = self.pairs[s]
            base = s * STRIP
            left = tuple(ref[a - base : b - base, :width] for ref in (high, low))
            right = tuple(ref[c - base : d - base, :width] for ref in (high, low))
            part = product(left, right, ROWS_ROWS)
            total = part if total is None else total + part
        return total


def tiles_of(a, b, size=2 * BLOCK):
    return [(r, min(r + size, b)) for r in range(a, b, size)]


def factor_columns(first, last, rows, scale, mine, theirs, damping, panels, state, extra):
    column, corner, inverse, work, upper = state
    row = lax.broadcasted_iota(jnp.int32, (BLOCK, BLOCK), 0)
    col = lax.broadcasted_iota(jnp.int32, (BLOCK, BLOCK), 1)

    def gram(k, a, b):
        s, c = divmod(k * BLOCK, STRIP)
        part = (slice(a - s * STRIP, b - s * STRIP), slice(c, c + BLOCK))
        s -= first * BLOCK // STRIP
        value = (mine[s][part] + theirs[s][part]) * scale
        if a == k * BLOCK:
            ids = lax.broadcasted_iota(jnp.int32, (b - a, BLOCK), 0)
            across = lax.broadcasted_iota(jnp.int32, (b - a, BLOCK), 1)
            value = value + jnp.where(ids == across, damping[:, a : a + BLOCK], 0.0)
        return value

    def below(k, a, b):
        pair = (inverse[k % 2, 0], inverse[k % 2, 1])
        panels.put(k, a, b, halves(product(halves(column[k % 2, a:b, :]), pair, ROWS_ROWS)))

    def fill(k, a, b, count):
        value = gram(k, a, b)
        if count:
            value = value - panels.sums(a, b, k * BLOCK, (k + 1) * BLOCK, count)
        return value

    def fill_column(k, a, b):
        column[k % 2, a:b, :] = fill(k, a, b, k)

    def fill_corner(k):
        corner[...] = fill(k, k * BLOCK, (k + 1) * BLOCK, k - 1)

    diagonal = fill(first, first * BLOCK, (first + 1) * BLOCK, first)
    for k in range(first, last):
        at, end = k * BLOCK, (k + 1) * BLOCK
        calls = []
        for a, b in tiles_of(end, rows):
            if k > first:
                calls.append(functools.partial(below, k - 1, a, b))
            calls.append(functools.partial(fill_column, k, a, b))
        if k + 1 < last:
            calls.insert(min(2, len(calls)), functools.partial(fill_corner, k + 1))
        factor_block(diagonal, work, upper, calls + extra(k))
        pair = halves(upper[:, BLOCK:])
        inverse[k % 2, 0] = pair[0]
        inverse[k % 2, 1] = pair[1]
        if k + 1 < last:
            beneath = halves(product(halves(column[k % 2, end : end + BLOCK, :]), pair, ROWS_ROWS))
            diagonal = corner[...] - product(beneath, beneath, ROWS_ROWS)
            panels.put(k, end, end + BLOCK, beneath)
        panels.put(k, at, end, halves(jnp.where(row >= col, upper[:, :BLOCK].T, 0.0)))
        above = at - at % STRIP
        if above < at:
            zero = jnp.zeros((at - above, BLOCK), jnp.bfloat16)
            panels.put(k, above, at, (zero, zero))
    for a, b in tiles_of(last * BLOCK, rows):
        below(last - 1, a, b)


def start_body(cell_total, damping, mine, theirs, high, low, *state):
    factor_columns(
        0, STRIP // BLOCK, high.shape[0], 1.0 / cell_total, [mine], [theirs], damping,
        Panels([(high, low)]), state, lambda k: [],
    )


def finish_body(chosen_cols, cell_total, count, place, damping, order, high, low, *refs):
    mine, refs = refs[:count], refs[count:]
    theirs, refs = refs[:count], refs[count:]
    trailing, factor, refs = refs[0], refs[1], refs[2:]
    state, row_hot, pairs = refs[:5], refs[5], refs[6:]
    rows = order.shape[1]
    scale = 1.0 / cell_total
    pairs = [(high, low)] + list(zip(pairs[::2], pairs[1::2]))
    group_rows, tile_cols = trailing.shape

    def place_rows():
        row_hot[...] = (
            place[0] + lax.broadcasted_iota(jnp.int32, (group_rows, rows), 0) == order[...]
        ).astype(jnp.bfloat16)
        trailing[...] = jnp.zeros_like(trailing)

    def col_hot(a, b):
        return (
            place[1] + lax.broadcasted_iota(jnp.int32, (tile_cols, b - a), 0) == order[:, a:b]
        ).astype(jnp.bfloat16)

    def emit(s):
        at, end = s * STRIP, (s + 1) * STRIP
        high, low = pairs[s]
        rows_high = dot(row_hot[:, at:], high[...], PLAIN)
        rows_low = dot(row_hot[:, at:], low[...], PLAIN)
        factor[:, at:end] = rows_high + rows_low
        kept = jnp.sum(row_hot[:, chosen_cols:].astype(jnp.float32), axis=1, keepdims=True)
        picks = col_hot(chosen_cols, rows)
        cols_high = dot(picks, high[chosen_cols - at :, :], PLAIN)
        cols_low = dot(picks, low[chosen_cols - at :, :], PLAIN)
        trailing[...] -= product(
            ((rows_high * kept).astype(jnp.bfloat16), (rows_low * kept).astype(jnp.bfloat16)),
            (cols_high.astype(jnp.bfloat16), cols_low.astype(jnp.bfloat16)),
            ROWS_ROWS,
        )

    def remain(at, end):
        ids = lax.broadcasted_iota(jnp.int32, (rows - at, end - at), 0)
        across = lax.broadcasted_iota(jnp.int32, (rows - at, end - at), 1)
        s = at // STRIP - 1
        strip = (mine[s][...] + theirs[s][...]) * scale
        strip = strip + jnp.where(ids == across, damping[:, at:end], 0.0)
        for value in halves(strip):
            some = dot(row_hot[:, at:], value, PLAIN).astype(jnp.bfloat16)
            trailing[...] += dot(some, col_hot(at, end), ROWS_ROWS)
            if end < rows:
                some = dot(row_hot[:, at:end], value[end - at :, :], ROWS_ROWS).astype(jnp.bfloat16)
                trailing[...] += dot(some, col_hot(end, rows), ROWS_ROWS)

    last = chosen_cols // BLOCK
    per = STRIP // BLOCK
    calls = {k: [] for k in range(per, last)}
    calls[per].append(place_rows)
    for s in range(len(pairs) - 1):
        calls[min((s + 1) * per + 1, last - 1)].append(functools.partial(emit, s))
    for i, (at, end) in enumerate((a, b) for a, b in strips_of(rows) if a >= chosen_cols):
        calls[max(per + 1, last - 1 - i % 2 * per)].append(functools.partial(remain, at, end))
    factor_columns(
        per, last, rows, scale, mine, theirs, damping, Panels(pairs), state, lambda k: calls[k]
    )
    emit(len(pairs) - 1)


def shards(
    tx_fields, rx_fields, layer_of_cell, layer_cond, tx_of_row, rx_of_row, damping, panel_order
):
    grp_count = lax.axis_size("grp")
    tile_count = lax.axis_size("tile")
    tile_cells = tx_fields.shape[1]
    ntx, nrx = tx_fields.shape[0], rx_fields.shape[0]
    rows = tx_of_row.shape[0]
    group_rows = rows // grp_count
    tile_cols = rows // tile_count
    chosen_cols = PANEL * NPAN
    grp, tile = lax.axis_index("grp"), lax.axis_index("tile")

    half = tile_cells // 2
    start = (grp % 2) * half

    def piece(x):
        return lax.dynamic_slice_in_dim(x, start, half, axis=x.ndim - 1)

    own = jnp.concatenate(
        [
            piece(tx_fields),
            piece(rx_fields),
            jnp.broadcast_to(piece(layer_of_cell).astype(jnp.bfloat16)[None, :], (PAD, half)),
        ],
        axis=0,
    )

    inner = 1
    while inner * inner * 4 <= tile_count:
        inner *= 2
    outer = tile_count // inner

    def along(value, step):
        pairs = []
        for i in range(tile_count):
            o, n = divmod(i, inner)
            o = o ^ step[0] if outer & (outer - 1) == 0 else (o + step[0]) % outer
            n = n ^ step[1] if inner & (inner - 1) == 0 else (n + step[1]) % inner
            pairs.append((i, o * inner + n))
        return lax.ppermute(value, "tile", pairs)

    near = [along(own, (0, k)) for k in range(1, inner)]
    far = [along(own, (k, 0)) for k in range(1, outer)]
    relayed = [[along(far[0], (0, k)) for k in range(1, inner)]]

    line = lambda x: x[None, :]
    width = -(-(ntx + nrx + 3) // BLOCK) * BLOCK
    hot, damp = pl.pallas_call(
        functools.partial(select_body, ntx, nrx),
        in_specs=[VMEM] * 4,
        out_specs=[VMEM] * 2,
        out_shape=[
            jax.ShapeDtypeStruct((rows, width), jnp.bfloat16),
            jax.ShapeDtypeStruct((1, rows), jnp.float32),
        ],
        scratch_shapes=[pltpu.VMEM((width, rows), jnp.bfloat16)],
        compiler_params=pltpu.CompilerParams(
            vmem_limit_bytes=grant(((rows, width), 8), ((rows, STRIP), 8))
        ),
        cost_estimate=pl.CostEstimate(
            flops=2 * width * rows * rows, bytes_accessed=4 * rows * width, transcendentals=0
        ),
    )(line(panel_order), line(tx_of_row), line(rx_of_row), line(damping))

    strips = strips_of(rows)
    strip_shapes = [jax.ShapeDtypeStruct((rows - a, b - a), jnp.float32) for a, b in strips]
    lower = sum((rows - a) * (b - a) for a, b in strips)
    conds = jnp.broadcast_to(layer_cond[:, None], (layer_cond.shape[0], BLOCK))

    def swap(value):
        return lax.ppermute(value, "grp", [(i, i ^ 1) for i in range(grp_count)])

    def add(blocks, sums, some=None):
        count = len(blocks)
        stacked = count > GROUP
        depth = half * (1 if stacked else min(count, GROUP))
        args = [jnp.stack(blocks)] if stacked else blocks
        chosen = strips[:some]
        cost = 2 * count * half * (sum((rows - a) * (b - a) for a, b in chosen) + rows * STRIP * 2)
        sens = jax.ShapeDtypeStruct((rows, depth), jnp.bfloat16)
        kept = some is not None
        return pl.pallas_call(
            functools.partial(gram_body, ntx, nrx, count, stacked, not sums, some),
            in_specs=[VMEM] * (2 + len(args) + len(sums[:some])),
            out_specs=[VMEM] * (len(chosen) + kept),
            out_shape=strip_shapes[:some] + [sens] * kept,
            scratch_shapes=[] if kept else [pltpu.VMEM(sens.shape, sens.dtype)],
            input_output_aliases={2 + len(args) + i: i for i in range(len(sums[:some]))},
            compiler_params=pltpu.CompilerParams(
                vmem_limit_bytes=grant(
                    ((lower,), 8), ((rows, depth), 2), ((rows, width), 2), ((count, own.size), 2)
                )
            ),
            cost_estimate=pl.CostEstimate(
                flops=cost, bytes_accessed=8 * lower, transcendentals=0
            ),
        )(hot, conds, *args, *sums[:some])

    sums = list(add([own] + near + far[:1], []))
    held = lax.optimization_barrier((tuple(far[1:]), tuple(sums)))
    far, sums = far[:1] + list(held[0]), list(held[1])
    relayed += [[along(value, (0, k)) for k in range(1, inner)] for value in far[1:]]
    sums = list(add(far[1:] + relayed[0], sums))
    blocks = [value for values in relayed[1:] for value in values]
    if len(blocks) > GROUP:
        sums = list(add(blocks, sums))
        theirs = [swap(sums[0])]
    else:
        one, sens = add(blocks, sums, 1)
        theirs = [swap(one)]
        others = strips[1:]
        sums = [one] + list(
            pl.pallas_call(
                functools.partial(rest_body, sens.shape[1], others),
                in_specs=[VMEM] * (1 + len(others)),
                out_specs=[VMEM] * len(others),
                out_shape=strip_shapes[1:],
                input_output_aliases={1 + i: i for i in range(len(others))},
                compiler_params=pltpu.CompilerParams(
                    vmem_limit_bytes=grant(((lower,), 8), (sens.shape, 2))
                ),
                cost_estimate=pl.CostEstimate(
                    flops=2 * lower * sens.shape[1], bytes_accessed=8 * lower, transcendentals=0
                ),
            )(sens, *sums[1:])
        )
    theirs += [swap(value) for value in sums[1:]]

    state = [
        pltpu.VMEM((2, rows, BLOCK), jnp.float32),
        pltpu.VMEM((BLOCK, BLOCK), jnp.float32),
        pltpu.VMEM((2, 2, BLOCK, BLOCK), jnp.bfloat16),
        pltpu.VMEM((BLOCK, 2 * BLOCK), jnp.float32),
        pltpu.VMEM((BLOCK, 2 * BLOCK), jnp.float32),
    ]
    cell_total = tile_cells * tile_count
    high, low = pl.pallas_call(
        functools.partial(start_body, cell_total),
        in_specs=[VMEM] * 3,
        out_specs=[VMEM] * 2,
        out_shape=[jax.ShapeDtypeStruct((rows, STRIP), jnp.bfloat16)] * 2,
        scratch_shapes=state,
        compiler_params=pltpu.CompilerParams(
            vmem_limit_bytes=grant(((rows, STRIP), 12), ((rows, BLOCK), 8), ((rows, STRIP), 8))
        ),
        cost_estimate=pl.CostEstimate(
            flops=rows * STRIP * cell_total, bytes_accessed=8 * rows * STRIP, transcendentals=0
        ),
    )(damp, sums[0], theirs[0])

    place = jnp.stack([grp * group_rows, tile * tile_cols]).astype(jnp.int32)
    later = [(rows - a, STRIP) for a in range(STRIP, chosen_cols, STRIP)]
    return tuple(
        pl.pallas_call(
            functools.partial(finish_body, chosen_cols, cell_total, len(strips) - 1),
            in_specs=[SMEM] + [VMEM] * (2 + 2 * len(strips)),
            out_specs=[VMEM, VMEM],
            out_shape=[
                jax.ShapeDtypeStruct((group_rows, tile_cols), jnp.float32),
                jax.ShapeDtypeStruct((group_rows, chosen_cols), jnp.float32),
            ],
            scratch_shapes=state
            + [pltpu.VMEM((group_rows, rows), jnp.bfloat16)]
            + [pltpu.VMEM(shape, jnp.bfloat16) for shape in later for _ in range(2)],
            compiler_params=pltpu.CompilerParams(
                vmem_limit_bytes=grant(
                    ((lower,), 8), ((rows, chosen_cols), 4), ((rows, BLOCK), 16),
                    ((group_rows, chosen_cols + STRIP), 4), ((group_rows, rows), 4),
                )
            ),
            cost_estimate=pl.CostEstimate(
                flops=6 * rows * rows * chosen_cols, bytes_accessed=8 * lower, transcendentals=0
            ),
        )(place, damp, line(panel_order), high, low, *sums[1:], *theirs[1:])
    )


def solution(mesh):
    placed = (P(None, "tile"), P(None, "tile"), P("tile"), P(), P(), P(), P(), P())
    return jax.shard_map(
        shards,
        mesh=mesh,
        in_specs=placed,
        out_specs=(P("grp", "tile"), P("grp", None)),
        check_vma=False,
    )
```

```python
import functools

import jax
import jax.numpy as jnp
from jax import lax
from jax.experimental import pallas as pl
from jax.experimental.pallas import tpu as pltpu
from jax.sharding import PartitionSpec as P

PANEL = 512
NPAN = 2
BLOCK = 128
STEP = 16
STRIP = 256
PARTS = 4
GROUP = 3
PAD = 16
VMEM = pl.BlockSpec(memory_space=pltpu.VMEM)
SMEM = pl.BlockSpec(memory_space=pltpu.SMEM)
ROWS_ROWS = ((1,), (1,))
PLAIN = ((1,), (0,))


def grant(*shapes):
    total = 0
    for shape, width in shapes:
        size = width
        for axis in shape:
            size *= axis
        total += size
    return min(60 * 2**20, total + total // 8 + 6 * 2**20)


def halves(value):
    high = value.astype(jnp.bfloat16)
    low = (value - high.astype(jnp.float32)).astype(jnp.bfloat16)
    return high, low


def dot(a, b, dims):
    return lax.dot_general(a, b, (dims, ((), ())), preferred_element_type=jnp.float32)


def product(left, right, dims):
    return dot(left[0], right[0], dims) + (dot(left[0], right[1], dims) + dot(left[1], right[0], dims))


def factor_block(block, work, upper, beside=()):
    size = block.shape[0]
    row = lax.broadcasted_iota(jnp.int32, (size, size), 0)
    col = lax.broadcasted_iota(jnp.int32, (size, size), 1)
    eye = (row == col).astype(jnp.float32)
    work[:, :size] = block
    work[:, size:] = eye
    sub = lax.broadcasted_iota(jnp.int32, (STEP, size), 0)
    wide = (STEP, size)
    rows0, rows1 = block[:STEP, :], eye[:STEP, :]
    for at in range(0, size, STEP):
        cols = [jnp.broadcast_to(rows0[:, at + k : at + k + 1], wide) for k in range(STEP)]
        for call in beside[at * len(beside) // size : (at + STEP) * len(beside) // size]:
            call()
        more = at + STEP < size
        if more:
            after = work[at + STEP : at + 2 * STEP, :]
            after_cols = [jnp.broadcast_to(after[:, at + k : at + k + 1], wide) for k in range(STEP)]
        done0 = done1 = jnp.zeros(wide, jnp.float32)
        for j in range(STEP):
            pivot = jnp.broadcast_to(cols[j][j : j + 1, :], wide)
            ratio = (cols[j] - jnp.where(sub == j, 1.0, 0.0)) * (1.0 / pivot)
            root = lax.rsqrt(pivot)
            row0 = jnp.broadcast_to(rows0[j : j + 1, :], wide)
            row1 = jnp.broadcast_to(rows1[j : j + 1, :], wide)
            done0 = jnp.where(sub == j, row0 * root, done0)
            done1 = jnp.where(sub == j, row1 * root, done1)
            rows0 = rows0 - ratio * row0
            rows1 = rows1 - ratio * row1
            for k in range(j + 1, STEP):
                cols[k] = cols[k] - ratio * jnp.broadcast_to(cols[k][j : j + 1, :], wide)
        upper[at : at + STEP, :size] = done0
        upper[at : at + STEP, size:] = done1
        if not more:
            break
        terms0 = [after_cols[k] * jnp.broadcast_to(rows0[k : k + 1, :], wide) for k in range(STEP)]
        terms1 = [after_cols[k] * jnp.broadcast_to(rows1[k : k + 1, :], wide) for k in range(STEP)]
        while len(terms0) > 1:
            terms0 = [a + b for a, b in zip(terms0[::2], terms0[1::2])]
            terms1 = [a + b for a, b in zip(terms1[::2], terms1[1::2])]
        if at + 2 * STEP < size:
            solved = jnp.concatenate([rows0, rows1], axis=1)
            parts = [solved, jnp.zeros((size - at - STEP, 2 * size), jnp.float32)]
            if at > 0:
                parts.insert(0, jnp.zeros((at, 2 * size), jnp.float32))
            rest = work[at + 2 * STEP :, :]
            work[at + 2 * STEP :, :] = rest - product(
                halves(rest[:, :size]), halves(jnp.concatenate(parts, axis=0)), PLAIN
            )
        rows0 = after[:, :size] - terms0[0]
        rows1 = after[:, size:] - terms1[0]


def strips_of(rows):
    return [(a, min(a + STRIP, rows)) for a in range(0, rows, STRIP)]


def select_body(ntx, nrx, order, tx_of_row, rx_of_row, damping, hot, damp, line, table):
    rows = order.shape[0]
    table[:ntx, :] = (
        lax.broadcasted_iota(jnp.int32, (ntx, rows), 0) == tx_of_row[...].reshape(1, rows)
    ).astype(jnp.bfloat16)
    table[ntx : ntx + nrx, :] = (
        lax.broadcasted_iota(jnp.int32, (nrx, rows), 0) == rx_of_row[...].reshape(1, rows)
    ).astype(jnp.bfloat16)
    line[...] = order[...].reshape(1, rows)
    spare = table.shape[0] - ntx - nrx
    damping = damping[...].reshape(1, rows)
    high = damping.astype(jnp.bfloat16).astype(jnp.float32)
    middle, low = halves(damping - high)
    which = lax.broadcasted_iota(jnp.int32, (spare, rows), 0)
    table[ntx + nrx :, :] = (
        jnp.where(which == 0, high, 0.0)
        + jnp.where(which == 1, middle.astype(jnp.float32), 0.0)
        + jnp.where(which == 2, low.astype(jnp.float32), 0.0)
    ).astype(jnp.bfloat16)
    for a, b in strips_of(rows):
        pick = (
            lax.broadcasted_iota(jnp.int32, (rows, b - a), 0) == line[:, a:b]
        ).astype(jnp.bfloat16)
        found = dot(table[...], pick, PLAIN)
        hot[a:b, :] = found.T.astype(jnp.bfloat16)
        damp[:, a:b] = jnp.sum(found[ntx + nrx :, :], axis=0, keepdims=True)


def rest_body(depth, strips, sens, *refs):
    for s, (a, b) in enumerate(strips):
        refs[len(strips) + s][...] = refs[s][...] + dot(sens[a:, :], sens[a:b, :], ROWS_ROWS)


def gram_body(ntx, nrx, count, stacked, first, some, hot, layer_cond, *refs):
    held = 1 if stacked else count
    blocks, refs = refs[:held], refs[held:]
    rows = hot.shape[0]
    bands = strips_of(rows)
    strips = bands[:some]
    before = () if first else refs[: len(strips)]
    after = refs[len(before) : len(before) + len(strips)]
    sens, conds = refs[-2:]
    nlayer = layer_cond.shape[0]
    size = blocks[0].shape[-1]

    def conductivities(cells, at):
        layer = cells[ntx + nrx : ntx + nrx + 1, :].astype(jnp.float32)
        level = lax.broadcasted_iota(jnp.int32, (nlayer, size), 0).astype(jnp.float32)
        cond = jnp.sum(jnp.where(level == layer, layer_cond[:, :1], 0.0), axis=0, keepdims=True)
        conds[at // size] = cond

    def fill(group):
        part = rows // PARTS

        def some(i, carry):
            here = pl.ds(pl.multiple_of(i * part, 16), part)
            for g, cells in enumerate(group):
                tx = dot(hot[here, :ntx], cells[:ntx, :], PLAIN)
                rx = dot(hot[here, ntx : ntx + nrx], cells[ntx : ntx + nrx, :], PLAIN)
                sens[here, g * size : (g + 1) * size] = (tx * rx * conds[g]).astype(jnp.bfloat16)
            return carry

        lax.fori_loop(0, PARTS, some, 0)

    def add(source, depth):
        for s, (a, b) in enumerate(strips):
            part = dot(sens[a:, :depth], sens[a:b, :depth], ROWS_ROWS)
            after[s][...] = part if source is None else source[s][...] + part

    if stacked:
        for s in range(len(strips)):
            after[s][...] = jnp.zeros_like(after[s]) if first else before[s][...]

        def one(i, carry):
            conductivities(blocks[0].at[i], 0)
            fill([blocks[0].at[i]])
            add(after, size)
            return carry

        lax.fori_loop(0, count, one, 0)
        return
    source = None if first else before
    for start in range(0, count, GROUP):
        group = blocks[start : start + GROUP]
        for i, cells in enumerate(group):
            conductivities(cells, i * size)
        fill(group)
        add(source, len(group) * size)
        source = after


class Panels:
    def __init__(self, pairs):
        self.pairs = pairs

    def of(self, k, a, b):
        s, c = divmod(k * BLOCK, STRIP)
        part = (slice(a - s * STRIP, b - s * STRIP), slice(c, c + BLOCK))
        return tuple(ref.at[part] for ref in self.pairs[s])

    def put(self, k, a, b, pair):
        for ref, value in zip(self.of(k, a, b), pair):
            ref[...] = value

    def sums(self, a, b, c, d, count):
        total = None
        for start in range(0, count * BLOCK, STRIP):
            s, width = start // STRIP, min(STRIP, count * BLOCK - start)
            high, low = self.pairs[s]
            base = s * STRIP
            left = tuple(ref[a - base : b - base, :width] for ref in (high, low))
            right = tuple(ref[c - base : d - base, :width] for ref in (high, low))
            part = product(left, right, ROWS_ROWS)
            total = part if total is None else total + part
        return total


def tiles_of(a, b, size=2 * BLOCK):
    return [(r, min(r + size, b)) for r in range(a, b, size)]


def factor_columns(first, last, rows, scale, mine, theirs, damping, panels, state, extra):
    column, corner, inverse, work, upper = state
    row = lax.broadcasted_iota(jnp.int32, (BLOCK, BLOCK), 0)
    col = lax.broadcasted_iota(jnp.int32, (BLOCK, BLOCK), 1)

    def gram(k, a, b):
        s, c = divmod(k * BLOCK, STRIP)
        part = (slice(a - s * STRIP, b - s * STRIP), slice(c, c + BLOCK))
        s -= first * BLOCK // STRIP
        value = (mine[s][part] + theirs[s][part]) * scale
        if a == k * BLOCK:
            ids = lax.broadcasted_iota(jnp.int32, (b - a, BLOCK), 0)
            across = lax.broadcasted_iota(jnp.int32, (b - a, BLOCK), 1)
            value = value + jnp.where(ids == across, damping[:, a : a + BLOCK], 0.0)
        return value

    def below(k, a, b):
        pair = (inverse[k % 2, 0], inverse[k % 2, 1])
        panels.put(k, a, b, halves(product(halves(column[k % 2, a:b, :]), pair, ROWS_ROWS)))

    def fill(k, a, b, count):
        value = gram(k, a, b)
        if count:
            value = value - panels.sums(a, b, k * BLOCK, (k + 1) * BLOCK, count)
        return value

    def fill_column(k, a, b):
        column[k % 2, a:b, :] = fill(k, a, b, k)

    def fill_corner(k):
        corner[...] = fill(k, k * BLOCK, (k + 1) * BLOCK, k - 1)

    diagonal = fill(first, first * BLOCK, (first + 1) * BLOCK, first)
    for k in range(first, last):
        at, end = k * BLOCK, (k + 1) * BLOCK
        calls = []
        for a, b in tiles_of(end, rows):
            if k > first:
                calls.append(functools.partial(below, k - 1, a, b))
            calls.append(functools.partial(fill_column, k, a, b))
        if k + 1 < last:
            calls.insert(min(2, len(calls)), functools.partial(fill_corner, k + 1))
        factor_block(diagonal, work, upper, calls + extra(k))
        pair = halves(upper[:, BLOCK:])
        inverse[k % 2, 0] = pair[0]
        inverse[k % 2, 1] = pair[1]
        if k + 1 < last:
            beneath = halves(product(halves(column[k % 2, end : end + BLOCK, :]), pair, ROWS_ROWS))
            diagonal = corner[...] - product(beneath, beneath, ROWS_ROWS)
            panels.put(k, end, end + BLOCK, beneath)
        panels.put(k, at, end, halves(jnp.where(row >= col, upper[:, :BLOCK].T, 0.0)))
        above = at - at % STRIP
        if above < at:
            zero = jnp.zeros((at - above, BLOCK), jnp.bfloat16)
            panels.put(k, above, at, (zero, zero))
    for a, b in tiles_of(last * BLOCK, rows):
        below(last - 1, a, b)


def start_body(cell_total, damping, mine, theirs, high, low, *state):
    factor_columns(
        0, STRIP // BLOCK, high.shape[0], 1.0 / cell_total, [mine], [theirs], damping,
        Panels([(high, low)]), state, lambda k: [],
    )


def finish_body(chosen_cols, cell_total, count, place, damping, order, high, low, *refs):
    mine, refs = refs[:count], refs[count:]
    theirs, refs = refs[:count], refs[count:]
    trailing, factor, refs = refs[0], refs[1], refs[2:]
    state, row_hot, pairs = refs[:5], refs[5], refs[6:]
    rows = order.shape[1]
    scale = 1.0 / cell_total
    pairs = [(high, low)] + list(zip(pairs[::2], pairs[1::2]))
    tile_cols, group_rows = trailing.shape

    def place_rows():
        row_hot[...] = (
            place[0] + lax.broadcasted_iota(jnp.int32, (group_rows, rows), 0) == order[...]
        ).astype(jnp.bfloat16)
        trailing[...] = jnp.zeros_like(trailing)

    def col_hot(a, b):
        return (
            place[1] + lax.broadcasted_iota(jnp.int32, (tile_cols, b - a), 0) == order[:, a:b]
        ).astype(jnp.bfloat16)

    def emit(s):
        at, end = s * STRIP, (s + 1) * STRIP
        high, low = pairs[s]
        rows_high = dot(row_hot[:, at:], high[...], PLAIN)
        rows_low = dot(row_hot[:, at:], low[...], PLAIN)
        factor[:, at:end] = rows_high + rows_low
        kept = jnp.sum(row_hot[:, chosen_cols:].astype(jnp.float32), axis=1, keepdims=True)
        picks = col_hot(chosen_cols, rows)
        cols_high = dot(picks, high[chosen_cols - at :, :], PLAIN)
        cols_low = dot(picks, low[chosen_cols - at :, :], PLAIN)
        trailing[...] -= product(
            (cols_high.astype(jnp.bfloat16), cols_low.astype(jnp.bfloat16)),
            ((rows_high * kept).astype(jnp.bfloat16), (rows_low * kept).astype(jnp.bfloat16)),
            ROWS_ROWS,
        )

    def remain(at, end):
        ids = lax.broadcasted_iota(jnp.int32, (rows - at, end - at), 0)
        across = lax.broadcasted_iota(jnp.int32, (rows - at, end - at), 1)
        s = at // STRIP - 1
        strip = (mine[s][...] + theirs[s][...]) * scale
        strip = strip + jnp.where(ids == across, damping[:, at:end], 0.0)
        for value in halves(strip):
            some = dot(row_hot[:, at:], value, PLAIN).astype(jnp.bfloat16)
            trailing[...] += dot(col_hot(at, end), some, ROWS_ROWS)
            if end < rows:
                some = dot(row_hot[:, at:end], value[end - at :, :], ROWS_ROWS).astype(jnp.bfloat16)
                trailing[...] += dot(col_hot(end, rows), some, ROWS_ROWS)

    last = chosen_cols // BLOCK
    per = STRIP // BLOCK
    calls = {k: [] for k in range(per, last)}
    calls[per].append(place_rows)
    for s in range(len(pairs) - 1):
        calls[min((s + 1) * per + 1, last - 1)].append(functools.partial(emit, s))
    for i, (at, end) in enumerate((a, b) for a, b in strips_of(rows) if a >= chosen_cols):
        calls[max(per + 1, last - 1 - i % 2 * per)].append(functools.partial(remain, at, end))
    factor_columns(
        per, last, rows, scale, mine, theirs, damping, Panels(pairs), state, lambda k: calls[k]
    )
    emit(len(pairs) - 1)


def shards(
    tx_fields, rx_fields, layer_of_cell, layer_cond, tx_of_row, rx_of_row, damping, panel_order
):
    grp_count = lax.axis_size("grp")
    tile_count = lax.axis_size("tile")
    tile_cells = tx_fields.shape[1]
    ntx, nrx = tx_fields.shape[0], rx_fields.shape[0]
    rows = tx_of_row.shape[0]
    group_rows = rows // grp_count
    tile_cols = rows // tile_count
    chosen_cols = PANEL * NPAN
    grp, tile = lax.axis_index("grp"), lax.axis_index("tile")

    half = tile_cells // 2
    start = (grp % 2) * half

    def piece(x):
        return lax.dynamic_slice_in_dim(x, start, half, axis=x.ndim - 1)

    own = jnp.concatenate(
        [
            piece(tx_fields),
            piece(rx_fields),
            jnp.broadcast_to(piece(layer_of_cell).astype(jnp.bfloat16)[None, :], (PAD, half)),
        ],
        axis=0,
    )

    inner = 1
    while inner * inner * 4 <= tile_count:
        inner *= 2
    outer = tile_count // inner

    def along(value, step):
        pairs = []
        for i in range(tile_count):
            o, n = divmod(i, inner)
            o = o ^ step[0] if outer & (outer - 1) == 0 else (o + step[0]) % outer
            n = n ^ step[1] if inner & (inner - 1) == 0 else (n + step[1]) % inner
            pairs.append((i, o * inner + n))
        return lax.ppermute(value, "tile", pairs)

    near = [along(own, (0, k)) for k in range(1, inner)]
    far = [along(own, (k, 0)) for k in range(1, outer)]
    relayed = [[along(far[0], (0, k)) for k in range(1, inner)]]

    width = -(-(ntx + nrx + 3) // BLOCK) * BLOCK
    hot, damp, order = pl.pallas_call(
        functools.partial(select_body, ntx, nrx),
        in_specs=[VMEM] * 4,
        out_specs=[VMEM] * 3,
        out_shape=[
            jax.ShapeDtypeStruct((rows, width), jnp.bfloat16),
            jax.ShapeDtypeStruct((1, rows), jnp.float32),
            jax.ShapeDtypeStruct((1, rows), jnp.int32),
        ],
        scratch_shapes=[pltpu.VMEM((width, rows), jnp.bfloat16)],
        compiler_params=pltpu.CompilerParams(
            vmem_limit_bytes=grant(((rows, width), 8), ((rows, STRIP), 8))
        ),
        cost_estimate=pl.CostEstimate(
            flops=2 * width * rows * rows, bytes_accessed=4 * rows * width, transcendentals=0
        ),
    )(panel_order, tx_of_row, rx_of_row, damping)

    strips = strips_of(rows)
    strip_shapes = [jax.ShapeDtypeStruct((rows - a, b - a), jnp.float32) for a, b in strips]
    lower = sum((rows - a) * (b - a) for a, b in strips)
    conds = jnp.broadcast_to(layer_cond[:, None], (layer_cond.shape[0], BLOCK))

    def swap(value):
        return lax.ppermute(value, "grp", [(i, i ^ 1) for i in range(grp_count)])

    def add(blocks, sums, some=None):
        count = len(blocks)
        stacked = count > GROUP
        depth = half * (1 if stacked else min(count, GROUP))
        args = [jnp.stack(blocks)] if stacked else blocks
        chosen = strips[:some]
        cost = 2 * count * half * (sum((rows - a) * (b - a) for a, b in chosen) + rows * STRIP * 2)
        sens = jax.ShapeDtypeStruct((rows, depth), jnp.bfloat16)
        kept = some is not None
        return pl.pallas_call(
            functools.partial(gram_body, ntx, nrx, count, stacked, not sums, some),
            in_specs=[VMEM] * (2 + len(args) + len(sums[:some])),
            out_specs=[VMEM] * (len(chosen) + kept),
            out_shape=strip_shapes[:some] + [sens] * kept,
            scratch_shapes=([] if kept else [pltpu.VMEM(sens.shape, sens.dtype)])
            + [pltpu.VMEM((GROUP, 1, half), jnp.float32)],
            input_output_aliases={2 + len(args) + i: i for i in range(len(sums[:some]))},
            compiler_params=pltpu.CompilerParams(
                vmem_limit_bytes=grant(
                    ((lower,), 8), ((rows, depth), 2), ((rows, width), 2), ((count, own.size), 2)
                )
            ),
            cost_estimate=pl.CostEstimate(
                flops=cost, bytes_accessed=8 * lower, transcendentals=0
            ),
        )(hot, conds, *args, *sums[:some])

    sums = list(add([own] + near + far[:1], []))
    held = lax.optimization_barrier((tuple(far[1:]), tuple(sums)))
    far, sums = far[:1] + list(held[0]), list(held[1])
    relayed += [[along(value, (0, k)) for k in range(1, inner)] for value in far[1:]]
    sums = list(add(far[1:] + relayed[0], sums))
    blocks = [value for values in relayed[1:] for value in values]
    if len(blocks) > GROUP:
        sums = list(add(blocks, sums))
        theirs = [swap(sums[0])]
    else:
        one, sens = add(blocks, sums, 1)
        theirs = [swap(one)]
        others = strips[1:]
        sums = [one] + list(
            pl.pallas_call(
                functools.partial(rest_body, sens.shape[1], others),
                in_specs=[VMEM] * (1 + len(others)),
                out_specs=[VMEM] * len(others),
                out_shape=strip_shapes[1:],
                input_output_aliases={1 + i: i for i in range(len(others))},
                compiler_params=pltpu.CompilerParams(
                    vmem_limit_bytes=grant(((lower,), 8), (sens.shape, 2))
                ),
                cost_estimate=pl.CostEstimate(
                    flops=2 * lower * sens.shape[1], bytes_accessed=8 * lower, transcendentals=0
                ),
            )(sens, *sums[1:])
        )
    theirs += [swap(value) for value in sums[1:]]

    state = [
        pltpu.VMEM((2, rows, BLOCK), jnp.float32),
        pltpu.VMEM((BLOCK, BLOCK), jnp.float32),
        pltpu.VMEM((2, 2, BLOCK, BLOCK), jnp.bfloat16),
        pltpu.VMEM((BLOCK, 2 * BLOCK), jnp.float32),
        pltpu.VMEM((BLOCK, 2 * BLOCK), jnp.float32),
    ]
    cell_total = tile_cells * tile_count
    high, low = pl.pallas_call(
        functools.partial(start_body, cell_total),
        in_specs=[VMEM] * 3,
        out_specs=[VMEM] * 2,
        out_shape=[jax.ShapeDtypeStruct((rows, STRIP), jnp.bfloat16)] * 2,
        scratch_shapes=state,
        compiler_params=pltpu.CompilerParams(
            vmem_limit_bytes=grant(((rows, STRIP), 12), ((rows, BLOCK), 8), ((rows, STRIP), 8))
        ),
        cost_estimate=pl.CostEstimate(
            flops=rows * STRIP * cell_total, bytes_accessed=8 * rows * STRIP, transcendentals=0
        ),
    )(damp, sums[0], theirs[0])

    place = jnp.stack([grp * group_rows, tile * tile_cols]).astype(jnp.int32)
    later = [(rows - a, STRIP) for a in range(STRIP, chosen_cols, STRIP)]
    trailing, factor = (
        pl.pallas_call(
            functools.partial(finish_body, chosen_cols, cell_total, len(strips) - 1),
            in_specs=[SMEM] + [VMEM] * (2 + 2 * len(strips)),
            out_specs=[VMEM, VMEM],
            out_shape=[
                jax.ShapeDtypeStruct((tile_cols, group_rows), jnp.float32),
                jax.ShapeDtypeStruct((group_rows, chosen_cols), jnp.float32),
            ],
            scratch_shapes=state
            + [pltpu.VMEM((group_rows, rows), jnp.bfloat16)]
            + [pltpu.VMEM(shape, jnp.bfloat16) for shape in later for _ in range(2)],
            compiler_params=pltpu.CompilerParams(
                vmem_limit_bytes=grant(
                    ((lower,), 8), ((rows, chosen_cols), 4), ((rows, BLOCK), 16),
                    ((group_rows, chosen_cols + STRIP), 4), ((group_rows, rows), 4),
                )
            ),
            cost_estimate=pl.CostEstimate(
                flops=6 * rows * rows * chosen_cols, bytes_accessed=8 * lower, transcendentals=0
            ),
        )(place, damp, order, high, low, *sums[1:], *theirs[1:])
    )
    return trailing.T, factor


def solution(mesh):
    placed = (P(None, "tile"), P(None, "tile"), P("tile"), P(), P(), P(), P(), P())
    return jax.shard_map(
        shards,
        mesh=mesh,
        in_specs=placed,
        out_specs=(P("grp", "tile"), P("grp", None)),
        check_vma=False,
    )
```

```python
import functools

import jax
import jax.numpy as jnp
from jax import lax
from jax.experimental import pallas as pl
from jax.experimental.pallas import tpu as pltpu
from jax.sharding import PartitionSpec as P

PANEL = 512
NPAN = 2
BLOCK = 128
STEP = 16
STRIP = 256
PARTS = 4
GROUP = 3
PAD = 16
VMEM = pl.BlockSpec(memory_space=pltpu.VMEM)
SMEM = pl.BlockSpec(memory_space=pltpu.SMEM)
ROWS_ROWS = ((1,), (1,))
PLAIN = ((1,), (0,))


def grant(*shapes):
    total = 0
    for shape, width in shapes:
        size = width
        for axis in shape:
            size *= axis
        total += size
    return min(60 * 2**20, total + total // 8 + 6 * 2**20)


def halves(value):
    high = value.astype(jnp.bfloat16)
    low = (value - high.astype(jnp.float32)).astype(jnp.bfloat16)
    return high, low


def dot(a, b, dims):
    return lax.dot_general(a, b, (dims, ((), ())), preferred_element_type=jnp.float32)


def product(left, right, dims):
    return dot(left[0], right[0], dims) + (dot(left[0], right[1], dims) + dot(left[1], right[0], dims))


def factor_block(block, work, upper, beside=()):
    size = block.shape[0]
    row = lax.broadcasted_iota(jnp.int32, (size, size), 0)
    col = lax.broadcasted_iota(jnp.int32, (size, size), 1)
    eye = (row == col).astype(jnp.float32)
    work[:, :size] = block
    work[:, size:] = eye
    sub = lax.broadcasted_iota(jnp.int32, (STEP, size), 0)
    wide = (STEP, size)
    rows0, rows1 = block[:STEP, :], eye[:STEP, :]
    for at in range(0, size, STEP):
        cols = [jnp.broadcast_to(rows0[:, at + k : at + k + 1], wide) for k in range(STEP)]
        for call in beside[at * len(beside) // size : (at + STEP) * len(beside) // size]:
            call()
        more = at + STEP < size
        if more:
            after = work[at + STEP : at + 2 * STEP, :]
            after_cols = [jnp.broadcast_to(after[:, at + k : at + k + 1], wide) for k in range(STEP)]
        done0 = done1 = jnp.zeros(wide, jnp.float32)
        for j in range(STEP):
            pivot = jnp.broadcast_to(cols[j][j : j + 1, :], wide)
            ratio = (cols[j] - jnp.where(sub == j, 1.0, 0.0)) * (1.0 / pivot)
            root = lax.rsqrt(pivot)
            row0 = jnp.broadcast_to(rows0[j : j + 1, :], wide)
            row1 = jnp.broadcast_to(rows1[j : j + 1, :], wide)
            done0 = jnp.where(sub == j, row0 * root, done0)
            done1 = jnp.where(sub == j, row1 * root, done1)
            rows0 = rows0 - ratio * row0
            rows1 = rows1 - ratio * row1
            for k in range(j + 1, STEP):
                cols[k] = cols[k] - ratio * jnp.broadcast_to(cols[k][j : j + 1, :], wide)
        upper[at : at + STEP, :size] = done0
        upper[at : at + STEP, size:] = done1
        if not more:
            break
        terms0 = [after_cols[k] * jnp.broadcast_to(rows0[k : k + 1, :], wide) for k in range(STEP)]
        terms1 = [after_cols[k] * jnp.broadcast_to(rows1[k : k + 1, :], wide) for k in range(STEP)]
        while len(terms0) > 1:
            terms0 = [a + b for a, b in zip(terms0[::2], terms0[1::2])]
            terms1 = [a + b for a, b in zip(terms1[::2], terms1[1::2])]
        if at + 2 * STEP < size:
            solved = jnp.concatenate([rows0, rows1], axis=1)
            parts = [solved, jnp.zeros((size - at - STEP, 2 * size), jnp.float32)]
            if at > 0:
                parts.insert(0, jnp.zeros((at, 2 * size), jnp.float32))
            rest = work[at + 2 * STEP :, :]
            work[at + 2 * STEP :, :] = rest - product(
                halves(rest[:, :size]), halves(jnp.concatenate(parts, axis=0)), PLAIN
            )
        rows0 = after[:, :size] - terms0[0]
        rows1 = after[:, size:] - terms1[0]


def strips_of(rows):
    return [(a, min(a + STRIP, rows)) for a in range(0, rows, STRIP)]


def own_body(tx_fields, rx_fields, layer_of_cell, out, layer, sems):
    ntx, nrx, half = tx_fields.shape[0], rx_fields.shape[0], out.shape[1]
    start = pl.multiple_of(lax.rem(lax.axis_index("grp"), 2) * half, half)
    copies = [
        pltpu.make_async_copy(layer_of_cell.at[pl.ds(start, half)], layer, sems.at[0]),
        pltpu.make_async_copy(tx_fields.at[:, pl.ds(start, half)], out.at[:ntx], sems.at[1]),
        pltpu.make_async_copy(
            rx_fields.at[:, pl.ds(start, half)], out.at[ntx : ntx + nrx], sems.at[2]
        ),
    ]
    for copy in copies:
        copy.start()
    copies[0].wait()
    line = layer[...].reshape(1, half).astype(jnp.float32)
    out[ntx + nrx :, :] = jnp.broadcast_to(line, (PAD, half)).astype(jnp.bfloat16)
    for copy in copies[1:]:
        copy.wait()


def select_body(
    ntx, nrx, order, tx_of_row, rx_of_row, damping, own, layer_cond, hot, damp, line, sens, table, ints, floats, sems
):
    rows = order.shape[0]
    copies = [
        pltpu.make_async_copy(source, target, sems.at[i])
        for i, (source, target) in enumerate(
            zip((order, tx_of_row, rx_of_row, damping), list(ints) + [floats])
        )
    ]
    for copy in copies:
        copy.start()
    for copy in copies:
        copy.wait()
    order, tx_of_row, rx_of_row = ints
    damping = floats
    table[:ntx, :] = (
        lax.broadcasted_iota(jnp.int32, (ntx, rows), 0) == tx_of_row[...].reshape(1, rows)
    ).astype(jnp.bfloat16)
    table[ntx : ntx + nrx, :] = (
        lax.broadcasted_iota(jnp.int32, (nrx, rows), 0) == rx_of_row[...].reshape(1, rows)
    ).astype(jnp.bfloat16)
    line[...] = order[...].reshape(1, rows)
    spare = table.shape[0] - ntx - nrx
    damping = damping[...].reshape(1, rows)
    high = damping.astype(jnp.bfloat16).astype(jnp.float32)
    middle, low = halves(damping - high)
    which = lax.broadcasted_iota(jnp.int32, (spare, rows), 0)
    table[ntx + nrx :, :] = (
        jnp.where(which == 0, high, 0.0)
        + jnp.where(which == 1, middle.astype(jnp.float32), 0.0)
        + jnp.where(which == 2, low.astype(jnp.float32), 0.0)
    ).astype(jnp.bfloat16)
    for a, b in strips_of(rows):
        pick = (
            lax.broadcasted_iota(jnp.int32, (rows, b - a), 0) == line[:, a:b]
        ).astype(jnp.bfloat16)
        found = dot(table[...], pick, PLAIN)
        hot[a:b, :] = found.T.astype(jnp.bfloat16)
        damp[:, a:b] = jnp.sum(found[ntx + nrx :, :], axis=0, keepdims=True)
    sensitivities(ntx, nrx, [own], [conductivities(ntx, nrx, own, layer_cond)], hot, sens)


def conductivities(ntx, nrx, cells, layer_cond):
    nlayer, size = layer_cond.shape[0], cells.shape[-1]
    layer = cells[ntx + nrx : ntx + nrx + 1, :].astype(jnp.float32)
    level = lax.broadcasted_iota(jnp.int32, (nlayer, size), 0).astype(jnp.float32)
    return jnp.sum(jnp.where(level == layer, layer_cond[:, :1], 0.0), axis=0, keepdims=True)


def sensitivities(ntx, nrx, group, conds, hot, sens, at=0):
    rows = hot.shape[0]
    part = rows // PARTS

    def some(i, carry):
        here = pl.ds(pl.multiple_of(i * part, 16), part)
        for g, cells in enumerate(group):
            size = cells.shape[-1]
            tx = dot(hot[here, :ntx], cells[:ntx, :], PLAIN)
            rx = dot(hot[here, ntx : ntx + nrx], cells[ntx : ntx + nrx, :], PLAIN)
            sens[here, at + g * size : at + (g + 1) * size] = (tx * rx * conds[g][...]).astype(jnp.bfloat16)
        return carry

    lax.fori_loop(0, PARTS, some, 0)


def rest_body(depth, strips, sens, *refs):
    for s, (a, b) in enumerate(strips):
        refs[len(strips) + s][...] = refs[s][...] + dot(sens[a:, :], sens[a:b, :], ROWS_ROWS)


def gram_body(ntx, nrx, count, stacked, first, some, hot, layer_cond, *refs):
    held = 1 + first if stacked else count
    blocks, refs = refs[:held], refs[held:]
    rows = hot.shape[0]
    strips = strips_of(rows)[:some]
    before = () if first else refs[: len(strips)]
    after = refs[len(before) : len(before) + len(strips)]
    sens, conds = refs[-2:]
    size = blocks[-1].shape[-1]

    def fill(group, at=0):
        for g, cells in enumerate(group):
            conds[g] = conductivities(ntx, nrx, cells, layer_cond)
        sensitivities(ntx, nrx, group, [conds.at[g] for g in range(len(group))], hot, sens, at)

    def add(source, depth):
        for s, (a, b) in enumerate(strips):
            part = dot(sens[a:, :depth], sens[a:b, :depth], ROWS_ROWS)
            after[s][...] = part if source is None else source[s][...] + part

    if stacked:
        if first:
            sens[...] = blocks[0][...]
            add(None, size)
        else:
            for s in range(len(strips)):
                after[s][...] = before[s][...]

        def one(i, carry):
            fill([blocks[-1].at[i]])
            add(after, size)
            return carry

        lax.fori_loop(0, count - first, one, 0)
        return
    if first:
        sens[:, :size] = blocks[0][...]
    fill(blocks[first:], size if first else 0)
    add(None if first else before, count * size)


class Panels:
    def __init__(self, pairs):
        self.pairs = pairs

    def of(self, k, a, b):
        s, c = divmod(k * BLOCK, STRIP)
        part = (slice(a - s * STRIP, b - s * STRIP), slice(c, c + BLOCK))
        return tuple(ref.at[part] for ref in self.pairs[s])

    def put(self, k, a, b, pair):
        for ref, value in zip(self.of(k, a, b), pair):
            ref[...] = value

    def sums(self, a, b, c, d, count):
        total = None
        for start in range(0, count * BLOCK, STRIP):
            s, width = start // STRIP, min(STRIP, count * BLOCK - start)
            high, low = self.pairs[s]
            base = s * STRIP
            left = tuple(ref[a - base : b - base, :width] for ref in (high, low))
            right = tuple(ref[c - base : d - base, :width] for ref in (high, low))
            part = product(left, right, ROWS_ROWS)
            total = part if total is None else total + part
        return total


def tiles_of(a, b, size=2 * BLOCK):
    return [(r, min(r + size, b)) for r in range(a, b, size)]


def factor_columns(first, last, rows, scale, mine, theirs, damping, panels, state, extra):
    column, corner, inverse, work, upper = state
    row = lax.broadcasted_iota(jnp.int32, (BLOCK, BLOCK), 0)
    col = lax.broadcasted_iota(jnp.int32, (BLOCK, BLOCK), 1)

    def gram(k, a, b):
        s, c = divmod(k * BLOCK, STRIP)
        part = (slice(a - s * STRIP, b - s * STRIP), slice(c, c + BLOCK))
        s -= first * BLOCK // STRIP
        value = (mine[s][part] + theirs[s][part]) * scale
        if a == k * BLOCK:
            ids = lax.broadcasted_iota(jnp.int32, (b - a, BLOCK), 0)
            across = lax.broadcasted_iota(jnp.int32, (b - a, BLOCK), 1)
            value = value + jnp.where(ids == across, damping[:, a : a + BLOCK], 0.0)
        return value

    def below(k, a, b):
        pair = (inverse[k % 2, 0], inverse[k % 2, 1])
        panels.put(k, a, b, halves(product(halves(column[k % 2, a:b, :]), pair, ROWS_ROWS)))

    def fill(k, a, b, count):
        value = gram(k, a, b)
        if count:
            value = value - panels.sums(a, b, k * BLOCK, (k + 1) * BLOCK, count)
        return value

    def fill_column(k, a, b):
        column[k % 2, a:b, :] = fill(k, a, b, k)

    def fill_corner(k):
        corner[...] = fill(k, k * BLOCK, (k + 1) * BLOCK, k - 1)

    diagonal = fill(first, first * BLOCK, (first + 1) * BLOCK, first)
    for k in range(first, last):
        at, end = k * BLOCK, (k + 1) * BLOCK
        calls = []
        for a, b in tiles_of(end, rows):
            if k > first:
                calls.append(functools.partial(below, k - 1, a, b))
            calls.append(functools.partial(fill_column, k, a, b))
        if k + 1 < last:
            calls.insert(min(2, len(calls)), functools.partial(fill_corner, k + 1))
        factor_block(diagonal, work, upper, calls + extra(k))
        pair = halves(upper[:, BLOCK:])
        inverse[k % 2, 0] = pair[0]
        inverse[k % 2, 1] = pair[1]
        if k + 1 < last:
            beneath = halves(product(halves(column[k % 2, end : end + BLOCK, :]), pair, ROWS_ROWS))
            diagonal = corner[...] - product(beneath, beneath, ROWS_ROWS)
            panels.put(k, end, end + BLOCK, beneath)
        panels.put(k, at, end, halves(jnp.where(row >= col, upper[:, :BLOCK].T, 0.0)))
        above = at - at % STRIP
        if above < at:
            zero = jnp.zeros((at - above, BLOCK), jnp.bfloat16)
            panels.put(k, above, at, (zero, zero))
    for a, b in tiles_of(last * BLOCK, rows):
        below(last - 1, a, b)


def start_body(cell_total, damping, mine, theirs, high, low, *state):
    factor_columns(
        0, STRIP // BLOCK, high.shape[0], 1.0 / cell_total, [mine], [theirs], damping,
        Panels([(high, low)]), state, lambda k: [],
    )


def finish_body(chosen_cols, cell_total, count, place, damping, order, high, low, *refs):
    mine, refs = refs[:count], refs[count:]
    theirs, refs = refs[:count], refs[count:]
    trailing, factor, refs = refs[0], refs[1], refs[2:]
    state, row_hot, pairs = refs[:5], refs[5], refs[6:]
    rows = order.shape[1]
    scale = 1.0 / cell_total
    pairs = [(high, low)] + list(zip(pairs[::2], pairs[1::2]))
    tile_cols, group_rows = trailing.shape

    def place_rows():
        row_hot[...] = (
            place[0] + lax.broadcasted_iota(jnp.int32, (group_rows, rows), 0) == order[...]
        ).astype(jnp.bfloat16)
        trailing[...] = jnp.zeros_like(trailing)

    def col_hot(a, b):
        return (
            place[1] + lax.broadcasted_iota(jnp.int32, (tile_cols, b - a), 0) == order[:, a:b]
        ).astype(jnp.bfloat16)

    def emit(s):
        at, end = s * STRIP, (s + 1) * STRIP
        high, low = pairs[s]
        rows_high = dot(row_hot[:, at:], high[...], PLAIN)
        rows_low = dot(row_hot[:, at:], low[...], PLAIN)
        factor[:, at:end] = rows_high + rows_low
        kept = jnp.sum(row_hot[:, chosen_cols:].astype(jnp.float32), axis=1, keepdims=True)
        picks = col_hot(chosen_cols, rows)
        cols_high = dot(picks, high[chosen_cols - at :, :], PLAIN)
        cols_low = dot(picks, low[chosen_cols - at :, :], PLAIN)
        trailing[...] -= product(
            (cols_high.astype(jnp.bfloat16), cols_low.astype(jnp.bfloat16)),
            ((rows_high * kept).astype(jnp.bfloat16), (rows_low * kept).astype(jnp.bfloat16)),
            ROWS_ROWS,
        )

    def remain(at, end):
        ids = lax.broadcasted_iota(jnp.int32, (rows - at, end - at), 0)
        across = lax.broadcasted_iota(jnp.int32, (rows - at, end - at), 1)
        s = at // STRIP - 1
        strip = (mine[s][...] + theirs[s][...]) * scale
        strip = strip + jnp.where(ids == across, damping[:, at:end], 0.0)
        for value in halves(strip):
            some = dot(row_hot[:, at:], value, PLAIN).astype(jnp.bfloat16)
            trailing[...] += dot(col_hot(at, end), some, ROWS_ROWS)
            if end < rows:
                some = dot(row_hot[:, at:end], value[end - at :, :], ROWS_ROWS).astype(jnp.bfloat16)
                trailing[...] += dot(col_hot(end, rows), some, ROWS_ROWS)

    last = chosen_cols // BLOCK
    per = STRIP // BLOCK
    calls = {k: [] for k in range(per, last)}
    calls[per].append(place_rows)
    for s in range(len(pairs) - 1):
        calls[min((s + 1) * per + 1, last - 1)].append(functools.partial(emit, s))
    for i, (at, end) in enumerate((a, b) for a, b in strips_of(rows) if a >= chosen_cols):
        calls[max(per + 1, last - 1 - i % 2 * per)].append(functools.partial(remain, at, end))
    factor_columns(
        per, last, rows, scale, mine, theirs, damping, Panels(pairs), state, lambda k: calls[k]
    )
    emit(len(pairs) - 1)


def shards(
    tx_fields, rx_fields, layer_of_cell, layer_cond, tx_of_row, rx_of_row, damping, panel_order
):
    grp_count = lax.axis_size("grp")
    tile_count = lax.axis_size("tile")
    tile_cells = tx_fields.shape[1]
    ntx, nrx = tx_fields.shape[0], rx_fields.shape[0]
    rows = tx_of_row.shape[0]
    group_rows = rows // grp_count
    tile_cols = rows // tile_count
    chosen_cols = PANEL * NPAN
    grp, tile = lax.axis_index("grp"), lax.axis_index("tile")

    half = tile_cells // 2
    own = pl.pallas_call(
        own_body,
        in_specs=[pl.BlockSpec(memory_space=pl.ANY)] * 3,
        out_specs=VMEM,
        out_shape=jax.ShapeDtypeStruct((ntx + nrx + PAD, half), jnp.bfloat16),
        scratch_shapes=[pltpu.VMEM((half,), jnp.int32), pltpu.SemaphoreType.DMA((3,))],
        compiler_params=pltpu.CompilerParams(vmem_limit_bytes=grant()),
    )(tx_fields, rx_fields, layer_of_cell)

    inner = 1
    while inner * inner * 4 <= tile_count:
        inner *= 2
    outer = tile_count // inner

    def along(value, step):
        pairs = []
        for i in range(tile_count):
            o, n = divmod(i, inner)
            o = o ^ step[0] if outer & (outer - 1) == 0 else (o + step[0]) % outer
            n = n ^ step[1] if inner & (inner - 1) == 0 else (n + step[1]) % inner
            pairs.append((i, o * inner + n))
        return lax.ppermute(value, "tile", pairs)

    near = [along(own, (0, k)) for k in range(1, inner)]
    far = [along(own, (k, 0)) for k in range(1, outer)]
    relayed = [[along(far[0], (0, k)) for k in range(1, inner)]]

    width = -(-(ntx + nrx + 3) // BLOCK) * BLOCK
    conds = jnp.broadcast_to(layer_cond[:, None], (layer_cond.shape[0], BLOCK))
    hot, damp, order, own_sens = pl.pallas_call(
        functools.partial(select_body, ntx, nrx),
        in_specs=[pl.BlockSpec(memory_space=pl.ANY)] * 4 + [VMEM] * 2,
        out_specs=[VMEM] * 4,
        out_shape=[
            jax.ShapeDtypeStruct((rows, width), jnp.bfloat16),
            jax.ShapeDtypeStruct((1, rows), jnp.float32),
            jax.ShapeDtypeStruct((1, rows), jnp.int32),
            jax.ShapeDtypeStruct((rows, half), jnp.bfloat16),
        ],
        scratch_shapes=[
            pltpu.VMEM((width, rows), jnp.bfloat16),
            [pltpu.VMEM((rows,), jnp.int32)] * 3,
            pltpu.VMEM((rows,), jnp.float32),
            pltpu.SemaphoreType.DMA((4,)),
        ],
        compiler_params=pltpu.CompilerParams(
            vmem_limit_bytes=grant(((rows, width), 8), ((rows, STRIP), 8), ((rows, half), 4))
        ),
        cost_estimate=pl.CostEstimate(
            flops=2 * width * rows * rows, bytes_accessed=4 * rows * width, transcendentals=0
        ),
    )(panel_order, tx_of_row, rx_of_row, damping, own, conds)

    strips = strips_of(rows)
    strip_shapes = [jax.ShapeDtypeStruct((rows - a, b - a), jnp.float32) for a, b in strips]
    lower = sum((rows - a) * (b - a) for a, b in strips)

    def swap(value):
        return lax.ppermute(value, "grp", [(i, i ^ 1) for i in range(grp_count)])

    def add(blocks, sums, some=None):
        count = len(blocks)
        stacked = count > GROUP
        depth = half * (1 if stacked else min(count, GROUP))
        begun = [] if sums else [own_sens]
        args = [jnp.stack(blocks[len(begun) :])] if stacked else blocks[len(begun) :]
        args = begun + args
        chosen = strips[:some]
        cost = 2 * count * half * (sum((rows - a) * (b - a) for a, b in chosen) + rows * STRIP * 2)
        sens = jax.ShapeDtypeStruct((rows, depth), jnp.bfloat16)
        kept = some is not None
        return pl.pallas_call(
            functools.partial(gram_body, ntx, nrx, count, stacked, not sums, some),
            in_specs=[VMEM] * (2 + len(args) + len(sums[:some])),
            out_specs=[VMEM] * (len(chosen) + kept),
            out_shape=strip_shapes[:some] + [sens] * kept,
            scratch_shapes=([] if kept else [pltpu.VMEM(sens.shape, sens.dtype)])
            + [pltpu.VMEM((GROUP, 1, half), jnp.float32)],
            compiler_params=pltpu.CompilerParams(
                vmem_limit_bytes=grant(
                    ((lower,), 8), ((rows, depth), 2), ((rows, width), 2), ((count, own.size), 2)
                )
            ),
            cost_estimate=pl.CostEstimate(
                flops=cost, bytes_accessed=8 * lower, transcendentals=0
            ),
        )(hot, conds, *args, *sums[:some])

    sums = list(add([own] + near + far[:1], []))
    held = lax.optimization_barrier((tuple(far[1:]), tuple(sums)))
    far, sums = far[:1] + list(held[0]), list(held[1])
    relayed += [[along(value, (0, k)) for k in range(1, inner)] for value in far[1:]]
    sums = list(add(far[1:] + relayed[0], sums))
    blocks = [value for values in relayed[1:] for value in values]
    if len(blocks) > GROUP:
        sums = list(add(blocks, sums))
        theirs = [swap(sums[0])]
    else:
        one, sens = add(blocks, sums, 1)
        theirs = [swap(one)]
        others = strips[1:]
        sums = [one] + list(
            pl.pallas_call(
                functools.partial(rest_body, sens.shape[1], others),
                in_specs=[VMEM] * (1 + len(others)),
                out_specs=[VMEM] * len(others),
                out_shape=strip_shapes[1:],
                compiler_params=pltpu.CompilerParams(
                    vmem_limit_bytes=grant(((lower,), 8), (sens.shape, 2))
                ),
                cost_estimate=pl.CostEstimate(
                    flops=2 * lower * sens.shape[1], bytes_accessed=8 * lower, transcendentals=0
                ),
            )(sens, *sums[1:])
        )
    theirs += [swap(value) for value in sums[1:]]

    state = [
        pltpu.VMEM((2, rows, BLOCK), jnp.float32),
        pltpu.VMEM((BLOCK, BLOCK), jnp.float32),
        pltpu.VMEM((2, 2, BLOCK, BLOCK), jnp.bfloat16),
        pltpu.VMEM((BLOCK, 2 * BLOCK), jnp.float32),
        pltpu.VMEM((BLOCK, 2 * BLOCK), jnp.float32),
    ]
    cell_total = tile_cells * tile_count
    high, low = pl.pallas_call(
        functools.partial(start_body, cell_total),
        in_specs=[VMEM] * 3,
        out_specs=[VMEM] * 2,
        out_shape=[jax.ShapeDtypeStruct((rows, STRIP), jnp.bfloat16)] * 2,
        scratch_shapes=state,
        compiler_params=pltpu.CompilerParams(
            vmem_limit_bytes=grant(((rows, STRIP), 12), ((rows, BLOCK), 8), ((rows, STRIP), 8))
        ),
        cost_estimate=pl.CostEstimate(
            flops=rows * STRIP * cell_total, bytes_accessed=8 * rows * STRIP, transcendentals=0
        ),
    )(damp, sums[0], theirs[0])

    place = jnp.stack([grp * group_rows, tile * tile_cols]).astype(jnp.int32)
    later = [(rows - a, STRIP) for a in range(STRIP, chosen_cols, STRIP)]
    trailing, factor = (
        pl.pallas_call(
            functools.partial(finish_body, chosen_cols, cell_total, len(strips) - 1),
            in_specs=[SMEM] + [VMEM] * (2 + 2 * len(strips)),
            out_specs=[VMEM, VMEM],
            out_shape=[
                jax.ShapeDtypeStruct((tile_cols, group_rows), jnp.float32),
                jax.ShapeDtypeStruct((group_rows, chosen_cols), jnp.float32),
            ],
            scratch_shapes=state
            + [pltpu.VMEM((group_rows, rows), jnp.bfloat16)]
            + [pltpu.VMEM(shape, jnp.bfloat16) for shape in later for _ in range(2)],
            compiler_params=pltpu.CompilerParams(
                vmem_limit_bytes=grant(
                    ((lower,), 8), ((rows, chosen_cols), 4), ((rows, BLOCK), 16),
                    ((group_rows, chosen_cols + STRIP), 4), ((group_rows, rows), 4),
                )
            ),
            cost_estimate=pl.CostEstimate(
                flops=6 * rows * rows * chosen_cols, bytes_accessed=8 * lower, transcendentals=0
            ),
        )(place, damp, order, high, low, *sums[1:], *theirs[1:])
    )
    return trailing.T, factor


def solution(mesh):
    placed = (P(None, "tile"), P(None, "tile"), P("tile"), P(), P(), P(), P(), P())
    return jax.shard_map(
        shards,
        mesh=mesh,
        in_specs=placed,
        out_specs=(P("grp", "tile"), P("grp", None)),
        check_vma=False,
    )
```

```python
import functools

import jax
import jax.numpy as jnp
from jax import lax
from jax.experimental import pallas as pl
from jax.experimental.pallas import tpu as pltpu
from jax.sharding import PartitionSpec as P

PANEL = 512
NPAN = 2
BLOCK = 128
STEP = 16
STRIP = 256
PARTS = 4
EMITS = 2
GROUP = 3
PAD = 16
VMEM = pl.BlockSpec(memory_space=pltpu.VMEM)
SMEM = pl.BlockSpec(memory_space=pltpu.SMEM)
ROWS_ROWS = ((1,), (1,))
PLAIN = ((1,), (0,))


def grant(*shapes):
    total = 0
    for shape, width in shapes:
        size = width
        for axis in shape:
            size *= axis
        total += size
    return min(60 * 2**20, total + total // 8 + 6 * 2**20)


def halves(value):
    high = value.astype(jnp.bfloat16)
    low = (value - high.astype(jnp.float32)).astype(jnp.bfloat16)
    return high, low


def dot(a, b, dims):
    return lax.dot_general(a, b, (dims, ((), ())), preferred_element_type=jnp.float32)


def product(left, right, dims):
    return dot(left[0], right[0], dims) + (dot(left[0], right[1], dims) + dot(left[1], right[0], dims))


def factor_block(block, work, upper, beside=()):
    size = block.shape[0]
    row = lax.broadcasted_iota(jnp.int32, (size, size), 0)
    col = lax.broadcasted_iota(jnp.int32, (size, size), 1)
    eye = (row == col).astype(jnp.float32)
    work[:, :size] = block
    work[:, size:] = eye
    sub = lax.broadcasted_iota(jnp.int32, (STEP, size), 0)
    wide = (STEP, size)
    rows0, rows1 = block[:STEP, :], eye[:STEP, :]
    for at in range(0, size, STEP):
        cols = [jnp.broadcast_to(rows0[:, at + k : at + k + 1], wide) for k in range(STEP)]
        for call in beside[at * len(beside) // size : (at + STEP) * len(beside) // size]:
            call()
        more = at + STEP < size
        if more:
            after = work[at + STEP : at + 2 * STEP, :]
            after_cols = [jnp.broadcast_to(after[:, at + k : at + k + 1], wide) for k in range(STEP)]
        done0 = done1 = jnp.zeros(wide, jnp.float32)
        for j in range(STEP):
            pivot = jnp.broadcast_to(cols[j][j : j + 1, :], wide)
            ratio = (cols[j] - jnp.where(sub == j, 1.0, 0.0)) * (1.0 / pivot)
            root = lax.rsqrt(pivot)
            row0 = jnp.broadcast_to(rows0[j : j + 1, :], wide)
            row1 = jnp.broadcast_to(rows1[j : j + 1, :], wide)
            done0 = jnp.where(sub == j, row0 * root, done0)
            done1 = jnp.where(sub == j, row1 * root, done1)
            rows0 = rows0 - ratio * row0
            rows1 = rows1 - ratio * row1
            for k in range(j + 1, STEP):
                cols[k] = cols[k] - ratio * jnp.broadcast_to(cols[k][j : j + 1, :], wide)
        upper[at : at + STEP, :size] = done0
        upper[at : at + STEP, size:] = done1
        if not more:
            break
        terms0 = [after_cols[k] * jnp.broadcast_to(rows0[k : k + 1, :], wide) for k in range(STEP)]
        terms1 = [after_cols[k] * jnp.broadcast_to(rows1[k : k + 1, :], wide) for k in range(STEP)]
        while len(terms0) > 1:
            terms0 = [a + b for a, b in zip(terms0[::2], terms0[1::2])]
            terms1 = [a + b for a, b in zip(terms1[::2], terms1[1::2])]
        if at + 2 * STEP < size:
            solved = jnp.concatenate([rows0, rows1], axis=1)
            parts = [solved, jnp.zeros((size - at - STEP, 2 * size), jnp.float32)]
            if at > 0:
                parts.insert(0, jnp.zeros((at, 2 * size), jnp.float32))
            rest = work[at + 2 * STEP :, :]
            work[at + 2 * STEP :, :] = rest - product(
                halves(rest[:, :size]), halves(jnp.concatenate(parts, axis=0)), PLAIN
            )
        rows0 = after[:, :size] - terms0[0]
        rows1 = after[:, size:] - terms1[0]


def strips_of(rows):
    return [(a, min(a + STRIP, rows)) for a in range(0, rows, STRIP)]


def own_body(tx_fields, rx_fields, layer_of_cell, out, layer, sems):
    ntx, nrx, half = tx_fields.shape[0], rx_fields.shape[0], out.shape[1]
    start = pl.multiple_of(lax.rem(lax.axis_index("grp"), 2) * half, half)
    copies = [
        pltpu.make_async_copy(layer_of_cell.at[pl.ds(start, half)], layer, sems.at[0]),
        pltpu.make_async_copy(tx_fields.at[:, pl.ds(start, half)], out.at[:ntx], sems.at[1]),
        pltpu.make_async_copy(
            rx_fields.at[:, pl.ds(start, half)], out.at[ntx : ntx + nrx], sems.at[2]
        ),
    ]
    for copy in copies:
        copy.start()
    copies[0].wait()
    line = layer[...].reshape(1, half).astype(jnp.float32)
    out[ntx + nrx :, :] = jnp.broadcast_to(line, (PAD, half)).astype(jnp.bfloat16)
    for copy in copies[1:]:
        copy.wait()


def select_body(
    ntx, nrx, vectors, damping, own, layer_cond, hot, damp, line, sens, table
):
    rows = vectors.shape[1]
    order, tx_of_row, rx_of_row = (vectors[i : i + 1, :] for i in range(3))
    damping = damping[...].reshape(1, rows)
    table[:ntx, :] = (
        lax.broadcasted_iota(jnp.int32, (ntx, rows), 0) == tx_of_row
    ).astype(jnp.bfloat16)
    table[ntx : ntx + nrx, :] = (
        lax.broadcasted_iota(jnp.int32, (nrx, rows), 0) == rx_of_row
    ).astype(jnp.bfloat16)
    line[...] = order
    spare = table.shape[0] - ntx - nrx
    high = damping.astype(jnp.bfloat16).astype(jnp.float32)
    middle, low = halves(damping - high)
    which = lax.broadcasted_iota(jnp.int32, (spare, rows), 0)
    table[ntx + nrx :, :] = (
        jnp.where(which == 0, high, 0.0)
        + jnp.where(which == 1, middle.astype(jnp.float32), 0.0)
        + jnp.where(which == 2, low.astype(jnp.float32), 0.0)
    ).astype(jnp.bfloat16)
    for a, b in strips_of(rows):
        pick = (
            lax.broadcasted_iota(jnp.int32, (rows, b - a), 0) == line[:, a:b]
        ).astype(jnp.bfloat16)
        found = dot(table[...], pick, PLAIN)
        hot[a:b, :] = found.T.astype(jnp.bfloat16)
        damp[:, a:b] = jnp.sum(found[ntx + nrx :, :], axis=0, keepdims=True)
    sensitivities(ntx, nrx, [own], [conductivities(ntx, nrx, own, layer_cond)], hot, sens)


def conductivities(ntx, nrx, cells, layer_cond):
    nlayer, size = layer_cond.shape[0], cells.shape[-1]
    layer = cells[ntx + nrx : ntx + nrx + 1, :].astype(jnp.float32)
    level = lax.broadcasted_iota(jnp.int32, (nlayer, size), 0).astype(jnp.float32)
    return jnp.sum(jnp.where(level == layer, layer_cond[:, :1], 0.0), axis=0, keepdims=True)


def sensitivities(ntx, nrx, group, conds, hot, sens, at=0):
    rows = hot.shape[0]
    part = rows // PARTS

    def some(i, carry):
        here = pl.ds(pl.multiple_of(i * part, 16), part)
        for g, cells in enumerate(group):
            size = cells.shape[-1]
            tx = dot(hot[here, :ntx], cells[:ntx, :], PLAIN)
            rx = dot(hot[here, ntx : ntx + nrx], cells[ntx : ntx + nrx, :], PLAIN)
            sens[here, at + g * size : at + (g + 1) * size] = (tx * rx * conds[g][...]).astype(jnp.bfloat16)
        return carry

    lax.fori_loop(0, PARTS, some, 0)


def rest_body(depth, strips, sens, *refs):
    for s, (a, b) in enumerate(strips):
        refs[len(strips) + s][...] = refs[s][...] + dot(sens[a:, :], sens[a:b, :], ROWS_ROWS)


def gram_body(ntx, nrx, count, stacked, first, some, hot, layer_cond, *refs):
    held = 1 + first if stacked else count
    blocks, refs = refs[:held], refs[held:]
    rows = hot.shape[0]
    strips = strips_of(rows)[:some]
    before = () if first else refs[: len(strips)]
    after = refs[len(before) : len(before) + len(strips)]
    sens, conds = refs[-2:]
    size = blocks[-1].shape[-1]

    def fill(group, at=0):
        for g, cells in enumerate(group):
            conds[g] = conductivities(ntx, nrx, cells, layer_cond)
        sensitivities(ntx, nrx, group, [conds.at[g] for g in range(len(group))], hot, sens, at)

    def add(source, depth):
        for s, (a, b) in enumerate(strips):
            part = dot(sens[a:, :depth], sens[a:b, :depth], ROWS_ROWS)
            after[s][...] = part if source is None else source[s][...] + part

    if stacked:
        if first:
            sens[...] = blocks[0][...]
            add(None, size)
        else:
            for s in range(len(strips)):
                after[s][...] = before[s][...]

        def one(i, carry):
            fill([blocks[-1].at[i]])
            add(after, size)
            return carry

        lax.fori_loop(0, count - first, one, 0)
        return
    if first:
        sens[:, :size] = blocks[0][...]
    fill(blocks[first:], size if first else 0)
    add(None if first else before, count * size)


class Panels:
    def __init__(self, pairs):
        self.pairs = pairs

    def of(self, k, a, b):
        s, c = divmod(k * BLOCK, STRIP)
        part = (slice(a - s * STRIP, b - s * STRIP), slice(c, c + BLOCK))
        return tuple(ref.at[part] for ref in self.pairs[s])

    def put(self, k, a, b, pair):
        for ref, value in zip(self.of(k, a, b), pair):
            ref[...] = value

    def sums(self, a, b, c, d, count):
        total = None
        for start in range(0, count * BLOCK, STRIP):
            s, width = start // STRIP, min(STRIP, count * BLOCK - start)
            high, low = self.pairs[s]
            base = s * STRIP
            left = tuple(ref[a - base : b - base, :width] for ref in (high, low))
            right = tuple(ref[c - base : d - base, :width] for ref in (high, low))
            part = product(left, right, ROWS_ROWS)
            total = part if total is None else total + part
        return total


def tiles_of(a, b, size=2 * BLOCK):
    return [(r, min(r + size, b)) for r in range(a, b, size)]


def factor_columns(first, last, rows, scale, mine, theirs, damping, panels, state, extra):
    column, corner, inverse, work, upper = state
    row = lax.broadcasted_iota(jnp.int32, (BLOCK, BLOCK), 0)
    col = lax.broadcasted_iota(jnp.int32, (BLOCK, BLOCK), 1)

    def gram(k, a, b):
        s, c = divmod(k * BLOCK, STRIP)
        part = (slice(a - s * STRIP, b - s * STRIP), slice(c, c + BLOCK))
        s -= first * BLOCK // STRIP
        value = (mine[s][part] + theirs[s][part]) * scale
        if a == k * BLOCK:
            ids = lax.broadcasted_iota(jnp.int32, (b - a, BLOCK), 0)
            across = lax.broadcasted_iota(jnp.int32, (b - a, BLOCK), 1)
            value = value + jnp.where(ids == across, damping[:, a : a + BLOCK], 0.0)
        return value

    def below(k, a, b):
        pair = (inverse[k % 2, 0], inverse[k % 2, 1])
        panels.put(k, a, b, halves(product(halves(column[k % 2, a:b, :]), pair, ROWS_ROWS)))

    def fill(k, a, b, count):
        value = gram(k, a, b)
        if count:
            value = value - panels.sums(a, b, k * BLOCK, (k + 1) * BLOCK, count)
        return value

    def fill_column(k, a, b):
        column[k % 2, a:b, :] = fill(k, a, b, k)

    def fill_corner(k):
        corner[...] = fill(k, k * BLOCK, (k + 1) * BLOCK, k - 1)

    diagonal = fill(first, first * BLOCK, (first + 1) * BLOCK, first)
    for k in range(first, last):
        at, end = k * BLOCK, (k + 1) * BLOCK
        calls = []
        for a, b in tiles_of(end, rows):
            if k > first:
                calls.append(functools.partial(below, k - 1, a, b))
            calls.append(functools.partial(fill_column, k, a, b))
        if k + 1 < last:
            calls.insert(min(2, len(calls)), functools.partial(fill_corner, k + 1))
        factor_block(diagonal, work, upper, calls + extra(k))
        pair = halves(upper[:, BLOCK:])
        inverse[k % 2, 0] = pair[0]
        inverse[k % 2, 1] = pair[1]
        if k + 1 < last:
            beneath = halves(product(halves(column[k % 2, end : end + BLOCK, :]), pair, ROWS_ROWS))
            diagonal = corner[...] - product(beneath, beneath, ROWS_ROWS)
            panels.put(k, end, end + BLOCK, beneath)
        panels.put(k, at, end, halves(jnp.where(row >= col, upper[:, :BLOCK].T, 0.0)))
        above = at - at % STRIP
        if above < at:
            zero = jnp.zeros((at - above, BLOCK), jnp.bfloat16)
            panels.put(k, above, at, (zero, zero))
    for a, b in tiles_of(last * BLOCK, rows):
        below(last - 1, a, b)


def start_body(cell_total, damping, mine, theirs, high, low, *state):
    factor_columns(
        0, STRIP // BLOCK, high.shape[0], 1.0 / cell_total, [mine], [theirs], damping,
        Panels([(high, low)]), state, lambda k: [],
    )


def finish_body(chosen_cols, cell_total, count, place, damping, order, high, low, *refs):
    mine, refs = refs[:count], refs[count:]
    theirs, refs = refs[:count], refs[count:]
    trailing, factor, refs = refs[0], refs[1], refs[2:]
    state, row_hot, rows_pairs, pairs = refs[:5], refs[5], refs[6], refs[7:]
    rows = order.shape[1]
    scale = 1.0 / cell_total
    pairs = [(high, low)] + list(zip(pairs[::2], pairs[1::2]))
    tile_cols, group_rows = trailing.shape

    def place_rows():
        row_hot[...] = (
            place[0] + lax.broadcasted_iota(jnp.int32, (group_rows, rows), 0) == order[...]
        ).astype(jnp.bfloat16)
        trailing[...] = jnp.zeros_like(trailing)

    def col_hot(a, b):
        return (
            place[1] + lax.broadcasted_iota(jnp.int32, (tile_cols, b - a), 0) == order[:, a:b]
        ).astype(jnp.bfloat16)

    def emit(s, part):
        at, end = s * STRIP, (s + 1) * STRIP
        high, low = pairs[s]
        size = group_rows // EMITS
        here = slice(part * size, (part + 1) * size)
        rows_high = dot(row_hot[here, at:], high[...], PLAIN)
        rows_low = dot(row_hot[here, at:], low[...], PLAIN)
        factor[here, at:end] = rows_high + rows_low
        kept = jnp.sum(row_hot[here, chosen_cols:].astype(jnp.float32), axis=1, keepdims=True)
        rows_pairs[0, here, :] = (rows_high * kept).astype(jnp.bfloat16)
        rows_pairs[1, here, :] = (rows_low * kept).astype(jnp.bfloat16)

    def subtract(s):
        high, low = pairs[s]
        at = s * STRIP
        picks = col_hot(chosen_cols, rows)
        cols_high = dot(picks, high[chosen_cols - at :, :], PLAIN)
        cols_low = dot(picks, low[chosen_cols - at :, :], PLAIN)
        trailing[...] -= product(
            (cols_high.astype(jnp.bfloat16), cols_low.astype(jnp.bfloat16)),
            (rows_pairs[0], rows_pairs[1]),
            ROWS_ROWS,
        )

    def remain(at, end):
        ids = lax.broadcasted_iota(jnp.int32, (rows - at, end - at), 0)
        across = lax.broadcasted_iota(jnp.int32, (rows - at, end - at), 1)
        s = at // STRIP - 1
        strip = (mine[s][...] + theirs[s][...]) * scale
        strip = strip + jnp.where(ids == across, damping[:, at:end], 0.0)
        for value in halves(strip):
            some = dot(row_hot[:, at:], value, PLAIN).astype(jnp.bfloat16)
            trailing[...] += dot(col_hot(at, end), some, ROWS_ROWS)
            if end < rows:
                some = dot(row_hot[:, at:end], value[end - at :, :], ROWS_ROWS).astype(jnp.bfloat16)
                trailing[...] += dot(col_hot(end, rows), some, ROWS_ROWS)

    last = chosen_cols // BLOCK
    per = STRIP // BLOCK
    calls = {k: [] for k in range(per, last)}
    calls[per].append(place_rows)
    for s in range(len(pairs) - 1):
        for part in range(EMITS):
            calls[min((s + 1) * per + 1, last - 1)].append(functools.partial(emit, s, part))
        calls[min((s + 1) * per + 1, last - 1)].append(functools.partial(subtract, s))
    for i, (at, end) in enumerate((a, b) for a, b in strips_of(rows) if a >= chosen_cols):
        calls[max(per + 1, last - 1 - i % 2 * per)].append(functools.partial(remain, at, end))
    factor_columns(
        per, last, rows, scale, mine, theirs, damping, Panels(pairs), state, lambda k: calls[k]
    )
    for part in range(EMITS):
        emit(len(pairs) - 1, part)
    subtract(len(pairs) - 1)


def shards(
    tx_fields, rx_fields, layer_of_cell, layer_cond, tx_of_row, rx_of_row, damping, panel_order
):
    grp_count = lax.axis_size("grp")
    tile_count = lax.axis_size("tile")
    tile_cells = tx_fields.shape[1]
    ntx, nrx = tx_fields.shape[0], rx_fields.shape[0]
    rows = tx_of_row.shape[0]
    group_rows = rows // grp_count
    tile_cols = rows // tile_count
    chosen_cols = PANEL * NPAN
    grp, tile = lax.axis_index("grp"), lax.axis_index("tile")

    half = tile_cells // 2
    own = pl.pallas_call(
        own_body,
        in_specs=[pl.BlockSpec(memory_space=pl.ANY)] * 3,
        out_specs=VMEM,
        out_shape=jax.ShapeDtypeStruct((ntx + nrx + PAD, half), jnp.bfloat16),
        scratch_shapes=[pltpu.VMEM((half,), jnp.int32), pltpu.SemaphoreType.DMA((3,))],
        compiler_params=pltpu.CompilerParams(vmem_limit_bytes=grant()),
    )(tx_fields, rx_fields, layer_of_cell)

    inner = 1
    while inner * inner * 4 <= tile_count:
        inner *= 2
    outer = tile_count // inner

    def along(value, step):
        pairs = []
        for i in range(tile_count):
            o, n = divmod(i, inner)
            o = o ^ step[0] if outer & (outer - 1) == 0 else (o + step[0]) % outer
            n = n ^ step[1] if inner & (inner - 1) == 0 else (n + step[1]) % inner
            pairs.append((i, o * inner + n))
        return lax.ppermute(value, "tile", pairs)

    vectors = jnp.stack([panel_order, tx_of_row, rx_of_row])
    near = [along(own, (0, k)) for k in range(1, inner)]
    far = [along(own, (k, 0)) for k in range(1, outer)]
    relayed = [[along(far[0], (0, k)) for k in range(1, inner)]]

    width = -(-(ntx + nrx + 3) // BLOCK) * BLOCK
    conds = jnp.broadcast_to(layer_cond[:, None], (layer_cond.shape[0], BLOCK))
    hot, damp, order, own_sens = pl.pallas_call(
        functools.partial(select_body, ntx, nrx),
        in_specs=[VMEM] * 4,
        out_specs=[VMEM] * 4,
        out_shape=[
            jax.ShapeDtypeStruct((rows, width), jnp.bfloat16),
            jax.ShapeDtypeStruct((1, rows), jnp.float32),
            jax.ShapeDtypeStruct((1, rows), jnp.int32),
            jax.ShapeDtypeStruct((rows, half), jnp.bfloat16),
        ],
        scratch_shapes=[pltpu.VMEM((width, rows), jnp.bfloat16)],
        compiler_params=pltpu.CompilerParams(
            vmem_limit_bytes=grant(((rows, width), 8), ((rows, STRIP), 8), ((rows, half), 4))
        ),
        cost_estimate=pl.CostEstimate(
            flops=2 * width * rows * rows, bytes_accessed=4 * rows * width, transcendentals=0
        ),
    )(vectors, damping, own, conds)

    strips = strips_of(rows)
    strip_shapes = [jax.ShapeDtypeStruct((rows - a, b - a), jnp.float32) for a, b in strips]
    lower = sum((rows - a) * (b - a) for a, b in strips)

    def swap(value):
        return lax.ppermute(value, "grp", [(i, i ^ 1) for i in range(grp_count)])

    def add(blocks, sums, some=None):
        count = len(blocks)
        stacked = count > GROUP
        depth = half * (1 if stacked else min(count, GROUP))
        begun = [] if sums else [own_sens]
        args = [jnp.stack(blocks[len(begun) :])] if stacked else blocks[len(begun) :]
        args = begun + args
        chosen = strips[:some]
        cost = 2 * count * half * (sum((rows - a) * (b - a) for a, b in chosen) + rows * STRIP * 2)
        sens = jax.ShapeDtypeStruct((rows, depth), jnp.bfloat16)
        kept = some is not None
        return pl.pallas_call(
            functools.partial(gram_body, ntx, nrx, count, stacked, not sums, some),
            in_specs=[VMEM] * (2 + len(args) + len(sums[:some])),
            out_specs=[VMEM] * (len(chosen) + kept),
            out_shape=strip_shapes[:some] + [sens] * kept,
            scratch_shapes=([] if kept else [pltpu.VMEM(sens.shape, sens.dtype)])
            + [pltpu.VMEM((GROUP, 1, half), jnp.float32)],
            compiler_params=pltpu.CompilerParams(
                vmem_limit_bytes=grant(
                    ((lower,), 8), ((rows, depth), 2), ((rows, width), 2), ((count, own.size), 2)
                )
            ),
            cost_estimate=pl.CostEstimate(
                flops=cost, bytes_accessed=8 * lower, transcendentals=0
            ),
        )(hot, conds, *args, *sums[:some])

    sums = list(add([own] + near + far[:1], []))
    held = lax.optimization_barrier((tuple(far[1:]), tuple(sums)))
    far, sums = far[:1] + list(held[0]), list(held[1])
    relayed += [[along(value, (0, k)) for k in range(1, inner)] for value in far[1:]]
    sums = list(add(far[1:] + relayed[0], sums))
    blocks = [value for values in relayed[1:] for value in values]
    if len(blocks) > GROUP:
        sums = list(add(blocks, sums))
        theirs = [swap(sums[0])]
    else:
        one, sens = add(blocks, sums, 1)
        theirs = [swap(one)]
        others = strips[1:]
        sums = [one] + list(
            pl.pallas_call(
                functools.partial(rest_body, sens.shape[1], others),
                in_specs=[VMEM] * (1 + len(others)),
                out_specs=[VMEM] * len(others),
                out_shape=strip_shapes[1:],
                compiler_params=pltpu.CompilerParams(
                    vmem_limit_bytes=grant(((lower,), 8), (sens.shape, 2))
                ),
                cost_estimate=pl.CostEstimate(
                    flops=2 * lower * sens.shape[1], bytes_accessed=8 * lower, transcendentals=0
                ),
            )(sens, *sums[1:])
        )
    theirs += [swap(value) for value in sums[1:]]

    state = [
        pltpu.VMEM((2, rows, BLOCK), jnp.float32),
        pltpu.VMEM((BLOCK, BLOCK), jnp.float32),
        pltpu.VMEM((2, 2, BLOCK, BLOCK), jnp.bfloat16),
        pltpu.VMEM((BLOCK, 2 * BLOCK), jnp.float32),
        pltpu.VMEM((BLOCK, 2 * BLOCK), jnp.float32),
    ]
    cell_total = tile_cells * tile_count
    high, low = pl.pallas_call(
        functools.partial(start_body, cell_total),
        in_specs=[VMEM] * 3,
        out_specs=[VMEM] * 2,
        out_shape=[jax.ShapeDtypeStruct((rows, STRIP), jnp.bfloat16)] * 2,
        scratch_shapes=state,
        compiler_params=pltpu.CompilerParams(
            vmem_limit_bytes=grant(((rows, STRIP), 12), ((rows, BLOCK), 8), ((rows, STRIP), 8))
        ),
        cost_estimate=pl.CostEstimate(
            flops=rows * STRIP * cell_total, bytes_accessed=8 * rows * STRIP, transcendentals=0
        ),
    )(damp, sums[0], theirs[0])

    place = jnp.stack([grp * group_rows, tile * tile_cols]).astype(jnp.int32)
    later = [(rows - a, STRIP) for a in range(STRIP, chosen_cols, STRIP)]
    trailing, factor = (
        pl.pallas_call(
            functools.partial(finish_body, chosen_cols, cell_total, len(strips) - 1),
            in_specs=[SMEM] + [VMEM] * (2 + 2 * len(strips)),
            out_specs=[VMEM, VMEM],
            out_shape=[
                jax.ShapeDtypeStruct((tile_cols, group_rows), jnp.float32),
                jax.ShapeDtypeStruct((group_rows, chosen_cols), jnp.float32),
            ],
            scratch_shapes=state
            + [pltpu.VMEM((group_rows, rows), jnp.bfloat16)]
            + [pltpu.VMEM((2, group_rows, STRIP), jnp.bfloat16)]
            + [pltpu.VMEM(shape, jnp.bfloat16) for shape in later for _ in range(2)],
            compiler_params=pltpu.CompilerParams(
                vmem_limit_bytes=grant(
                    ((lower,), 8), ((rows, chosen_cols), 4), ((rows, BLOCK), 16),
                    ((group_rows, chosen_cols + STRIP), 4), ((group_rows, rows), 4),
                )
            ),
            cost_estimate=pl.CostEstimate(
                flops=6 * rows * rows * chosen_cols, bytes_accessed=8 * lower, transcendentals=0
            ),
        )(place, damp, order, high, low, *sums[1:], *theirs[1:])
    )
    return trailing.T, factor


def solution(mesh):
    placed = (P(None, "tile"), P(None, "tile"), P("tile"), P(), P(), P(), P(), P())
    return jax.shard_map(
        shards,
        mesh=mesh,
        in_specs=placed,
        out_specs=(P("grp", "tile"), P("grp", None)),
        check_vma=False,
    )
```

```python
import functools

import jax
import jax.numpy as jnp
from jax import lax
from jax.experimental import pallas as pl
from jax.experimental.pallas import tpu as pltpu
from jax.sharding import PartitionSpec as P

PANEL = 512
NPAN = 2
BLOCK = 128
STEP = 16
STRIP = 256
PARTS = 4
EMITS = 2
GROUP = 3
PAD = 16
VMEM = pl.BlockSpec(memory_space=pltpu.VMEM)
SMEM = pl.BlockSpec(memory_space=pltpu.SMEM)
ROWS_ROWS = ((1,), (1,))
PLAIN = ((1,), (0,))


def grant(*shapes):
    total = 0
    for shape, width in shapes:
        size = width
        for axis in shape:
            size *= axis
        total += size
    return min(60 * 2**20, total + total // 8 + 6 * 2**20)


def halves(value):
    high = value.astype(jnp.bfloat16)
    low = (value - high.astype(jnp.float32)).astype(jnp.bfloat16)
    return high, low


def dot(a, b, dims):
    return lax.dot_general(a, b, (dims, ((), ())), preferred_element_type=jnp.float32)


def product(left, right, dims):
    return dot(left[0], right[0], dims) + (dot(left[0], right[1], dims) + dot(left[1], right[0], dims))


def factor_block(block, work, upper, beside=()):
    size = block.shape[0]
    row = lax.broadcasted_iota(jnp.int32, (size, size), 0)
    col = lax.broadcasted_iota(jnp.int32, (size, size), 1)
    eye = (row == col).astype(jnp.float32)
    work[:, :size] = block
    work[:, size:] = eye
    sub = lax.broadcasted_iota(jnp.int32, (STEP, size), 0)
    wide = (STEP, size)
    rows0, rows1 = block[:STEP, :], eye[:STEP, :]
    for at in range(0, size, STEP):
        cols = [jnp.broadcast_to(rows0[:, at + k : at + k + 1], wide) for k in range(STEP)]
        for call in beside[at * len(beside) // size : (at + STEP) * len(beside) // size]:
            call()
        more = at + STEP < size
        if more:
            after = work[at + STEP : at + 2 * STEP, :]
            after_cols = [jnp.broadcast_to(after[:, at + k : at + k + 1], wide) for k in range(STEP)]
        done0 = done1 = jnp.zeros(wide, jnp.float32)
        for j in range(STEP):
            pivot = jnp.broadcast_to(cols[j][j : j + 1, :], wide)
            ratio = (cols[j] - jnp.where(sub == j, 1.0, 0.0)) * (1.0 / pivot)
            root = lax.rsqrt(pivot)
            row0 = jnp.broadcast_to(rows0[j : j + 1, :], wide)
            row1 = jnp.broadcast_to(rows1[j : j + 1, :], wide)
            done0 = jnp.where(sub == j, row0 * root, done0)
            done1 = jnp.where(sub == j, row1 * root, done1)
            rows0 = rows0 - ratio * row0
            rows1 = rows1 - ratio * row1
            for k in range(j + 1, STEP):
                cols[k] = cols[k] - ratio * jnp.broadcast_to(cols[k][j : j + 1, :], wide)
        upper[at : at + STEP, :size] = done0
        upper[at : at + STEP, size:] = done1
        if not more:
            break
        terms0 = [after_cols[k] * jnp.broadcast_to(rows0[k : k + 1, :], wide) for k in range(STEP)]
        terms1 = [after_cols[k] * jnp.broadcast_to(rows1[k : k + 1, :], wide) for k in range(STEP)]
        while len(terms0) > 1:
            terms0 = [a + b for a, b in zip(terms0[::2], terms0[1::2])]
            terms1 = [a + b for a, b in zip(terms1[::2], terms1[1::2])]
        if at + 2 * STEP < size:
            solved = jnp.concatenate([rows0, rows1], axis=1)
            parts = [solved, jnp.zeros((size - at - STEP, 2 * size), jnp.float32)]
            if at > 0:
                parts.insert(0, jnp.zeros((at, 2 * size), jnp.float32))
            rest = work[at + 2 * STEP :, :]
            work[at + 2 * STEP :, :] = rest - product(
                halves(rest[:, :size]), halves(jnp.concatenate(parts, axis=0)), PLAIN
            )
        rows0 = after[:, :size] - terms0[0]
        rows1 = after[:, size:] - terms1[0]


def strips_of(rows):
    return [(a, min(a + STRIP, rows)) for a in range(0, rows, STRIP)]


def own_body(tx_fields, rx_fields, layer_of_cell, out, layer, sems):
    ntx, nrx, half = tx_fields.shape[0], rx_fields.shape[0], out.shape[1]
    start = pl.multiple_of(lax.rem(lax.axis_index("grp"), 2) * half, half)
    copies = [
        pltpu.make_async_copy(layer_of_cell.at[pl.ds(start, half)], layer, sems.at[0]),
        pltpu.make_async_copy(tx_fields.at[:, pl.ds(start, half)], out.at[:ntx], sems.at[1]),
        pltpu.make_async_copy(
            rx_fields.at[:, pl.ds(start, half)], out.at[ntx : ntx + nrx], sems.at[2]
        ),
    ]
    for copy in copies:
        copy.start()
    copies[0].wait()
    line = layer[...].reshape(1, half).astype(jnp.float32)
    out[ntx + nrx :, :] = jnp.broadcast_to(line, (PAD, half)).astype(jnp.bfloat16)
    for copy in copies[1:]:
        copy.wait()


def select_body(
    ntx, nrx, vectors, damping, own, layer_cond, hot, damp, line, sens, table
):
    rows = vectors.shape[1]
    order, tx_of_row, rx_of_row = (vectors[i : i + 1, :] for i in range(3))
    damping = damping[...].reshape(1, rows)
    table[:ntx, :] = (
        lax.broadcasted_iota(jnp.int32, (ntx, rows), 0) == tx_of_row
    ).astype(jnp.bfloat16)
    table[ntx : ntx + nrx, :] = (
        lax.broadcasted_iota(jnp.int32, (nrx, rows), 0) == rx_of_row
    ).astype(jnp.bfloat16)
    line[...] = order
    spare = table.shape[0] - ntx - nrx
    high = damping.astype(jnp.bfloat16).astype(jnp.float32)
    middle, low = halves(damping - high)
    which = lax.broadcasted_iota(jnp.int32, (spare, rows), 0)
    table[ntx + nrx :, :] = (
        jnp.where(which == 0, high, 0.0)
        + jnp.where(which == 1, middle.astype(jnp.float32), 0.0)
        + jnp.where(which == 2, low.astype(jnp.float32), 0.0)
    ).astype(jnp.bfloat16)
    for a, b in strips_of(rows):
        pick = (
            lax.broadcasted_iota(jnp.int32, (rows, b - a), 0) == line[:, a:b]
        ).astype(jnp.bfloat16)
        found = dot(table[...], pick, PLAIN)
        hot[a:b, :] = found.T.astype(jnp.bfloat16)
        damp[:, a:b] = jnp.sum(found[ntx + nrx :, :], axis=0, keepdims=True)
    sensitivities(ntx, nrx, [own], [conductivities(ntx, nrx, own, layer_cond)], hot, sens)


def conductivities(ntx, nrx, cells, layer_cond):
    nlayer, size = layer_cond.shape[0], cells.shape[-1]
    layer = cells[ntx + nrx : ntx + nrx + 1, :].astype(jnp.float32)
    level = lax.broadcasted_iota(jnp.int32, (nlayer, size), 0).astype(jnp.float32)
    return jnp.sum(jnp.where(level == layer, layer_cond[:, :1], 0.0), axis=0, keepdims=True)


def sensitivities(ntx, nrx, group, conds, hot, sens, at=0):
    rows = hot.shape[0]
    part = rows // PARTS

    def some(i, carry):
        here = pl.ds(pl.multiple_of(i * part, 16), part)
        for g, cells in enumerate(group):
            size = cells.shape[-1]
            tx = dot(hot[here, :ntx], cells[:ntx, :], PLAIN)
            rx = dot(hot[here, ntx : ntx + nrx], cells[ntx : ntx + nrx, :], PLAIN)
            sens[here, at + g * size : at + (g + 1) * size] = (tx * rx * conds[g][...]).astype(jnp.bfloat16)
        return carry

    lax.fori_loop(0, PARTS, some, 0)


def rest_body(depth, strips, sens, *refs):
    for s, (a, b) in enumerate(strips):
        refs[len(strips) + s][...] = refs[s][...] + dot(sens[a:, :], sens[a:b, :], ROWS_ROWS)


def sens_body(ntx, nrx, hot, layer_cond, cells, sens, cond):
    cond[...] = conductivities(ntx, nrx, cells, layer_cond)
    sensitivities(ntx, nrx, [cells], [cond], hot, sens)


def gram_body(ntx, nrx, count, stacked, first, begun, some, hot, layer_cond, *refs):
    held = 1 + first if stacked else count
    blocks, refs = refs[:held], refs[held:]
    rows = hot.shape[0]
    strips = strips_of(rows)[:some]
    before = () if first else refs[: len(strips)]
    after = refs[len(before) : len(before) + len(strips)]
    sens, conds = refs[-2:]
    size = blocks[-1].shape[-1]

    def fill(group, at=0):
        for g, cells in enumerate(group):
            conds[g] = conductivities(ntx, nrx, cells, layer_cond)
        sensitivities(ntx, nrx, group, [conds.at[g] for g in range(len(group))], hot, sens, at)

    def add(source, depth):
        for s, (a, b) in enumerate(strips):
            part = dot(sens[a:, :depth], sens[a:b, :depth], ROWS_ROWS)
            after[s][...] = part if source is None else source[s][...] + part

    if stacked:
        if first:
            sens[...] = blocks[0][...]
            add(None, size)
        else:
            for s in range(len(strips)):
                after[s][...] = before[s][...]

        def one(i, carry):
            fill([blocks[-1].at[i]])
            add(after, size)
            return carry

        lax.fori_loop(0, count - first, one, 0)
        return
    if begun:
        sens[:, :size] = blocks[0][...]
    fill(blocks[begun:], size if begun else 0)
    add(None if first else before, count * size)


class Panels:
    def __init__(self, pairs):
        self.pairs = pairs

    def of(self, k, a, b):
        s, c = divmod(k * BLOCK, STRIP)
        part = (slice(a - s * STRIP, b - s * STRIP), slice(c, c + BLOCK))
        return tuple(ref.at[part] for ref in self.pairs[s])

    def put(self, k, a, b, pair):
        for ref, value in zip(self.of(k, a, b), pair):
            ref[...] = value

    def sums(self, a, b, c, d, count):
        total = None
        for start in range(0, count * BLOCK, STRIP):
            s, width = start // STRIP, min(STRIP, count * BLOCK - start)
            high, low = self.pairs[s]
            base = s * STRIP
            left = tuple(ref[a - base : b - base, :width] for ref in (high, low))
            right = tuple(ref[c - base : d - base, :width] for ref in (high, low))
            part = product(left, right, ROWS_ROWS)
            total = part if total is None else total + part
        return total


def tiles_of(a, b, size=2 * BLOCK):
    return [(r, min(r + size, b)) for r in range(a, b, size)]


def factor_columns(first, last, rows, scale, mine, theirs, damping, panels, state, extra):
    column, corner, inverse, work, upper = state
    row = lax.broadcasted_iota(jnp.int32, (BLOCK, BLOCK), 0)
    col = lax.broadcasted_iota(jnp.int32, (BLOCK, BLOCK), 1)

    def gram(k, a, b):
        s, c = divmod(k * BLOCK, STRIP)
        part = (slice(a - s * STRIP, b - s * STRIP), slice(c, c + BLOCK))
        s -= first * BLOCK // STRIP
        value = (mine[s][part] + theirs[s][part]) * scale
        if a == k * BLOCK:
            ids = lax.broadcasted_iota(jnp.int32, (b - a, BLOCK), 0)
            across = lax.broadcasted_iota(jnp.int32, (b - a, BLOCK), 1)
            value = value + jnp.where(ids == across, damping[:, a : a + BLOCK], 0.0)
        return value

    def below(k, a, b):
        pair = (inverse[k % 2, 0], inverse[k % 2, 1])
        panels.put(k, a, b, halves(product(halves(column[k % 2, a:b, :]), pair, ROWS_ROWS)))

    def fill(k, a, b, count):
        value = gram(k, a, b)
        if count:
            value = value - panels.sums(a, b, k * BLOCK, (k + 1) * BLOCK, count)
        return value

    def fill_column(k, a, b):
        column[k % 2, a:b, :] = fill(k, a, b, k)

    def fill_corner(k):
        corner[...] = fill(k, k * BLOCK, (k + 1) * BLOCK, k - 1)

    diagonal = fill(first, first * BLOCK, (first + 1) * BLOCK, first)
    for k in range(first, last):
        at, end = k * BLOCK, (k + 1) * BLOCK
        calls = []
        for a, b in tiles_of(end, rows):
            if k > first:
                calls.append(functools.partial(below, k - 1, a, b))
            calls.append(functools.partial(fill_column, k, a, b))
        if k + 1 < last:
            calls.insert(min(2, len(calls)), functools.partial(fill_corner, k + 1))
        factor_block(diagonal, work, upper, calls + extra(k))
        pair = halves(upper[:, BLOCK:])
        inverse[k % 2, 0] = pair[0]
        inverse[k % 2, 1] = pair[1]
        if k + 1 < last:
            beneath = halves(product(halves(column[k % 2, end : end + BLOCK, :]), pair, ROWS_ROWS))
            diagonal = corner[...] - product(beneath, beneath, ROWS_ROWS)
            panels.put(k, end, end + BLOCK, beneath)
        panels.put(k, at, end, halves(jnp.where(row >= col, upper[:, :BLOCK].T, 0.0)))
        above = at - at % STRIP
        if above < at:
            zero = jnp.zeros((at - above, BLOCK), jnp.bfloat16)
            panels.put(k, above, at, (zero, zero))
    for a, b in tiles_of(last * BLOCK, rows):
        below(last - 1, a, b)


def start_body(cell_total, damping, mine, theirs, high, low, *state):
    factor_columns(
        0, STRIP // BLOCK, high.shape[0], 1.0 / cell_total, [mine], [theirs], damping,
        Panels([(high, low)]), state, lambda k: [],
    )


def finish_body(chosen_cols, cell_total, count, place, damping, order, high, low, *refs):
    mine, refs = refs[:count], refs[count:]
    theirs, refs = refs[:count], refs[count:]
    trailing, factor, refs = refs[0], refs[1], refs[2:]
    state, row_hot, rows_pairs, pairs = refs[:5], refs[5], refs[6], refs[7:]
    rows = order.shape[1]
    scale = 1.0 / cell_total
    pairs = [(high, low)] + list(zip(pairs[::2], pairs[1::2]))
    tile_cols, group_rows = trailing.shape

    def place_rows():
        row_hot[...] = (
            place[0] + lax.broadcasted_iota(jnp.int32, (group_rows, rows), 0) == order[...]
        ).astype(jnp.bfloat16)
        trailing[...] = jnp.zeros_like(trailing)

    def col_hot(a, b):
        return (
            place[1] + lax.broadcasted_iota(jnp.int32, (tile_cols, b - a), 0) == order[:, a:b]
        ).astype(jnp.bfloat16)

    def emit(s, part):
        at, end = s * STRIP, (s + 1) * STRIP
        high, low = pairs[s]
        size = group_rows // EMITS
        here = slice(part * size, (part + 1) * size)
        rows_high = dot(row_hot[here, at:], high[...], PLAIN)
        rows_low = dot(row_hot[here, at:], low[...], PLAIN)
        factor[here, at:end] = rows_high + rows_low
        kept = jnp.sum(row_hot[here, chosen_cols:].astype(jnp.float32), axis=1, keepdims=True)
        rows_pairs[0, here, :] = (rows_high * kept).astype(jnp.bfloat16)
        rows_pairs[1, here, :] = (rows_low * kept).astype(jnp.bfloat16)

    def subtract(s):
        high, low = pairs[s]
        at = s * STRIP
        picks = col_hot(chosen_cols, rows)
        cols_high = dot(picks, high[chosen_cols - at :, :], PLAIN)
        cols_low = dot(picks, low[chosen_cols - at :, :], PLAIN)
        trailing[...] -= product(
            (cols_high.astype(jnp.bfloat16), cols_low.astype(jnp.bfloat16)),
            (rows_pairs[0], rows_pairs[1]),
            ROWS_ROWS,
        )

    def remain(at, end):
        ids = lax.broadcasted_iota(jnp.int32, (rows - at, end - at), 0)
        across = lax.broadcasted_iota(jnp.int32, (rows - at, end - at), 1)
        s = at // STRIP - 1
        strip = (mine[s][...] + theirs[s][...]) * scale
        strip = strip + jnp.where(ids == across, damping[:, at:end], 0.0)
        for value in halves(strip):
            some = dot(row_hot[:, at:], value, PLAIN).astype(jnp.bfloat16)
            trailing[...] += dot(col_hot(at, end), some, ROWS_ROWS)
            if end < rows:
                some = dot(row_hot[:, at:end], value[end - at :, :], ROWS_ROWS).astype(jnp.bfloat16)
                trailing[...] += dot(col_hot(end, rows), some, ROWS_ROWS)

    last = chosen_cols // BLOCK
    per = STRIP // BLOCK
    calls = {k: [] for k in range(per, last)}
    calls[per].append(place_rows)
    for s in range(len(pairs) - 1):
        for part in range(EMITS):
            calls[min((s + 1) * per + 1, last - 1)].append(functools.partial(emit, s, part))
        calls[min((s + 1) * per + 1, last - 1)].append(functools.partial(subtract, s))
    for i, (at, end) in enumerate((a, b) for a, b in strips_of(rows) if a >= chosen_cols):
        calls[max(per + 1, last - 1 - i % 2 * per)].append(functools.partial(remain, at, end))
    factor_columns(
        per, last, rows, scale, mine, theirs, damping, Panels(pairs), state, lambda k: calls[k]
    )
    for part in range(EMITS):
        emit(len(pairs) - 1, part)
    subtract(len(pairs) - 1)


def shards(
    tx_fields, rx_fields, layer_of_cell, layer_cond, tx_of_row, rx_of_row, damping, panel_order
):
    grp_count = lax.axis_size("grp")
    tile_count = lax.axis_size("tile")
    tile_cells = tx_fields.shape[1]
    ntx, nrx = tx_fields.shape[0], rx_fields.shape[0]
    rows = tx_of_row.shape[0]
    group_rows = rows // grp_count
    tile_cols = rows // tile_count
    chosen_cols = PANEL * NPAN
    grp, tile = lax.axis_index("grp"), lax.axis_index("tile")

    half = tile_cells // 2
    own = pl.pallas_call(
        own_body,
        in_specs=[pl.BlockSpec(memory_space=pl.ANY)] * 3,
        out_specs=VMEM,
        out_shape=jax.ShapeDtypeStruct((ntx + nrx + PAD, half), jnp.bfloat16),
        scratch_shapes=[pltpu.VMEM((half,), jnp.int32), pltpu.SemaphoreType.DMA((3,))],
        compiler_params=pltpu.CompilerParams(vmem_limit_bytes=grant()),
    )(tx_fields, rx_fields, layer_of_cell)

    inner = 1
    while inner * inner * 4 <= tile_count:
        inner *= 2
    outer = tile_count // inner

    def along(value, step):
        pairs = []
        for i in range(tile_count):
            o, n = divmod(i, inner)
            o = o ^ step[0] if outer & (outer - 1) == 0 else (o + step[0]) % outer
            n = n ^ step[1] if inner & (inner - 1) == 0 else (n + step[1]) % inner
            pairs.append((i, o * inner + n))
        return lax.ppermute(value, "tile", pairs)

    vectors = jnp.stack([panel_order, tx_of_row, rx_of_row])
    near = [along(own, (0, k)) for k in range(1, inner)]
    far = [along(own, (k, 0)) for k in range(1, outer)]
    relayed = [[along(far[0], (0, k)) for k in range(1, inner)]]

    width = -(-(ntx + nrx + 3) // BLOCK) * BLOCK
    conds = jnp.broadcast_to(layer_cond[:, None], (layer_cond.shape[0], BLOCK))
    hot, damp, order, own_sens = pl.pallas_call(
        functools.partial(select_body, ntx, nrx),
        in_specs=[VMEM] * 4,
        out_specs=[VMEM] * 4,
        out_shape=[
            jax.ShapeDtypeStruct((rows, width), jnp.bfloat16),
            jax.ShapeDtypeStruct((1, rows), jnp.float32),
            jax.ShapeDtypeStruct((1, rows), jnp.int32),
            jax.ShapeDtypeStruct((rows, half), jnp.bfloat16),
        ],
        scratch_shapes=[pltpu.VMEM((width, rows), jnp.bfloat16)],
        compiler_params=pltpu.CompilerParams(
            vmem_limit_bytes=grant(((rows, width), 8), ((rows, STRIP), 8), ((rows, half), 4))
        ),
        cost_estimate=pl.CostEstimate(
            flops=2 * width * rows * rows, bytes_accessed=4 * rows * width, transcendentals=0
        ),
    )(vectors, damping, own, conds)

    strips = strips_of(rows)
    strip_shapes = [jax.ShapeDtypeStruct((rows - a, b - a), jnp.float32) for a, b in strips]
    lower = sum((rows - a) * (b - a) for a, b in strips)

    def swap(value):
        return lax.ppermute(value, "grp", [(i, i ^ 1) for i in range(grp_count)])

    def add(blocks, sums, some=None, begun=None):
        count = len(blocks)
        stacked = count > GROUP
        depth = half * (1 if stacked else min(count, GROUP))
        begun = [] if begun is None else [begun]
        args = [jnp.stack(blocks[len(begun) :])] if stacked else blocks[len(begun) :]
        args = begun + args
        chosen = strips[:some]
        cost = 2 * count * half * (sum((rows - a) * (b - a) for a, b in chosen) + rows * STRIP * 2)
        sens = jax.ShapeDtypeStruct((rows, depth), jnp.bfloat16)
        kept = some is not None
        return pl.pallas_call(
            functools.partial(gram_body, ntx, nrx, count, stacked, not sums, len(begun), some),
            in_specs=[VMEM] * (2 + len(args) + len(sums[:some])),
            out_specs=[VMEM] * (len(chosen) + kept),
            out_shape=strip_shapes[:some] + [sens] * kept,
            scratch_shapes=([] if kept else [pltpu.VMEM(sens.shape, sens.dtype)])
            + [pltpu.VMEM((GROUP, 1, half), jnp.float32)],
            compiler_params=pltpu.CompilerParams(
                vmem_limit_bytes=grant(
                    ((lower,), 8), ((rows, depth), 2), ((rows, width), 2), ((count, own.size), 2)
                )
            ),
            cost_estimate=pl.CostEstimate(
                flops=cost, bytes_accessed=8 * lower, transcendentals=0
            ),
        )(hot, conds, *args, *sums[:some])

    sums = list(add([own] + near + far[:1], [], begun=own_sens))
    held = lax.optimization_barrier((tuple(far[1:]), tuple(sums)))
    far, sums = far[:1] + list(held[0]), list(held[1])
    relayed += [[along(value, (0, k)) for k in range(1, inner)] for value in far[1:]]
    sums = list(add(far[1:] + relayed[0], sums))
    blocks = [value for values in relayed[1:] for value in values]
    if len(blocks) > GROUP:
        sums = list(add(blocks, sums))
        theirs = [swap(sums[0])]
    else:
        ready = pl.pallas_call(
            functools.partial(sens_body, ntx, nrx),
            in_specs=[VMEM] * 3,
            out_specs=VMEM,
            out_shape=jax.ShapeDtypeStruct((rows, half), jnp.bfloat16),
            scratch_shapes=[pltpu.VMEM((1, half), jnp.float32)],
            compiler_params=pltpu.CompilerParams(
                vmem_limit_bytes=grant(((rows, half), 4), ((rows, width), 2))
            ),
            cost_estimate=pl.CostEstimate(
                flops=4 * half * rows * STRIP, bytes_accessed=2 * rows * half, transcendentals=0
            ),
        )(hot, conds, blocks[0])
        one, sens = add(blocks, sums, 1, ready)
        theirs = [swap(one)]
        others = strips[1:]
        sums = [one] + list(
            pl.pallas_call(
                functools.partial(rest_body, sens.shape[1], others),
                in_specs=[VMEM] * (1 + len(others)),
                out_specs=[VMEM] * len(others),
                out_shape=strip_shapes[1:],
                compiler_params=pltpu.CompilerParams(
                    vmem_limit_bytes=grant(((lower,), 8), (sens.shape, 2))
                ),
                cost_estimate=pl.CostEstimate(
                    flops=2 * lower * sens.shape[1], bytes_accessed=8 * lower, transcendentals=0
                ),
            )(sens, *sums[1:])
        )
    theirs += [swap(value) for value in sums[1:]]

    state = [
        pltpu.VMEM((2, rows, BLOCK), jnp.float32),
        pltpu.VMEM((BLOCK, BLOCK), jnp.float32),
        pltpu.VMEM((2, 2, BLOCK, BLOCK), jnp.bfloat16),
        pltpu.VMEM((BLOCK, 2 * BLOCK), jnp.float32),
        pltpu.VMEM((BLOCK, 2 * BLOCK), jnp.float32),
    ]
    cell_total = tile_cells * tile_count
    high, low = pl.pallas_call(
        functools.partial(start_body, cell_total),
        in_specs=[VMEM] * 3,
        out_specs=[VMEM] * 2,
        out_shape=[jax.ShapeDtypeStruct((rows, STRIP), jnp.bfloat16)] * 2,
        scratch_shapes=state,
        compiler_params=pltpu.CompilerParams(
            vmem_limit_bytes=grant(((rows, STRIP), 12), ((rows, BLOCK), 8), ((rows, STRIP), 8))
        ),
        cost_estimate=pl.CostEstimate(
            flops=rows * STRIP * cell_total, bytes_accessed=8 * rows * STRIP, transcendentals=0
        ),
    )(damp, sums[0], theirs[0])

    place = jnp.stack([grp * group_rows, tile * tile_cols]).astype(jnp.int32)
    later = [(rows - a, STRIP) for a in range(STRIP, chosen_cols, STRIP)]
    trailing, factor = (
        pl.pallas_call(
            functools.partial(finish_body, chosen_cols, cell_total, len(strips) - 1),
            in_specs=[SMEM] + [VMEM] * (2 + 2 * len(strips)),
            out_specs=[VMEM, VMEM],
            out_shape=[
                jax.ShapeDtypeStruct((tile_cols, group_rows), jnp.float32),
                jax.ShapeDtypeStruct((group_rows, chosen_cols), jnp.float32),
            ],
            scratch_shapes=state
            + [pltpu.VMEM((group_rows, rows), jnp.bfloat16)]
            + [pltpu.VMEM((2, group_rows, STRIP), jnp.bfloat16)]
            + [pltpu.VMEM(shape, jnp.bfloat16) for shape in later for _ in range(2)],
            compiler_params=pltpu.CompilerParams(
                vmem_limit_bytes=grant(
                    ((lower,), 8), ((rows, chosen_cols), 4), ((rows, BLOCK), 16),
                    ((group_rows, chosen_cols + STRIP), 4), ((group_rows, rows), 4),
                )
            ),
            cost_estimate=pl.CostEstimate(
                flops=6 * rows * rows * chosen_cols, bytes_accessed=8 * lower, transcendentals=0
            ),
        )(place, damp, order, high, low, *sums[1:], *theirs[1:])
    )
    return trailing.T, factor


def solution(mesh):
    placed = (P(None, "tile"), P(None, "tile"), P("tile"), P(), P(), P(), P(), P())
    return jax.shard_map(
        shards,
        mesh=mesh,
        in_specs=placed,
        out_specs=(P("grp", "tile"), P("grp", None)),
        check_vma=False,
    )
```
